32 devices in a mesh: member: 4 (over z), cell: 8 (over y, x, core).
Axes of the slice: x: 2, y: 2, z: 4, core: 2. Of those that a mesh axis runs over, the one named last changes fastest.
Arguments:
- prior: float32 [64, 131072], P('member', 'cell')
- samples: float32 [64, 131072], P('member', 'cell')
- noise: float32 [2, 64, 131072], P(None, 'member', 'cell'), may hold values from -6 to 6
- obs_cells: int32 [2, 16384], P(None, 'cell'), may hold values from 0 to 131071, as said below
- obs_values: float32 [2, 16384], P(None, 'cell'), may hold values from -6 to 6
- seismic_mask: int32 [2, 1024], P(None, 'cell'), may hold values 0 or 1
Outputs:
- analysis: float32 [64, 131072], P('member', 'cell')
The draws below stay inside these ranges and needn't reach their ends.
Inputs may be any that keep to these rules, and one draw needn't show every extreme that they name: obs_cells[s, o] lies in cells k * 16384 to (k + 1) * 16384 - 1 where k = o // 2048; cells may repeat.
All inputs are finite; a program needn't handle non-finite values. No bound on the sum of `seismic_mask` on one device may be relied on, other than what follows from the above.
Results may differ from the reference program's by a relative error of at most 0.0003.
Values sent between devices are 32-bit elements; how exact they have to be, the bound alone decides.
A program may use at most 64 MiB of HBM per device.

```python
import math
import jax
import jax.numpy as jnp
from jax import lax

ENS = 64
C_DEV = 16384
SURVEYS = 2
STEPS = 2
NCELLS = 131072
OBS_DEV = 2048
OBS = 16384


def draw_prior(key, part):
    first, second = jax.random.split(key)
    where = jnp.arange(NCELLS, dtype=jnp.float32) / NCELLS
    rough = jax.random.uniform(first, (NCELLS,), jnp.float32, 0.7, 1.4)
    scale = 0.6 * jnp.exp(where * math.log(3.0)) * rough
    base = jax.random.normal(second, (ENS, NCELLS), jnp.float32)
    return base * scale[None, :]


def draw_samples(key, part):
    first = jax.random.fold_in(key, 0)
    base = jax.random.normal(first, (ENS, NCELLS), jnp.float32)
    return jnp.clip(base, -6.0, 6.0)


def draw_obs_cells(key, part):
    local = jax.random.randint(key, (SURVEYS, OBS), 0, C_DEV, dtype=jnp.int32)
    block = jnp.arange(OBS, dtype=jnp.int32) // OBS_DEV
    cells = local + block[None, :] * C_DEV
    cells = cells.at[0, 0].set(0)
    cells = cells.at[0, OBS - 1].set(NCELLS - 1)
    return cells


def plant(values, rng, low, top_value):
    extent = values.shape
    place = [jax.random.randint(jax.random.fold_in(rng, axis), (), 0, extent[axis]) for axis in range(len(extent))]
    values = values.at[tuple(place)].set(low)
    longest = extent.index(max(extent))
    place[longest] = (place[longest] + 1) % extent[longest]
    return values.at[tuple(place)].set(top_value)


def level_of(key, shape, shards, least, largest):
    level, own = 1.0, jax.random.fold_in(key, 6)
    for axis_at, parts in shards:
        steps = jnp.exp(jax.random.uniform(jax.random.fold_in(own, axis_at), (parts,), jnp.float32, least / len(shards), largest / len(shards)))
        level = level * jnp.repeat(steps, shape[axis_at] // parts).reshape([-1 if axis == axis_at else 1 for axis in range(len(shape))])
    return level


def scatter_about(rng, dims, deviation, bound, cuts=(), kind=jnp.bfloat16):
    values = jax.random.normal(rng, dims, jnp.float32) * deviation
    if len(cuts) > 0:
        values = level_of(rng, dims, cuts, -0.22, 0.18) * values
    return jnp.clip(values, min=-bound, max=bound).astype(kind)


def setup_inputs(seed: int = 0) -> dict:
    keys = jax.random.split(jax.random.key(seed), 7)
    return {
        "prior": draw_prior(jax.random.fold_in(keys[6], 71), 0),
        "samples": draw_samples(jax.random.fold_in(keys[6], 71), 0),
        "noise": scatter_about(keys[2], (STEPS, ENS, NCELLS), 1.0, 6.0, ((1, 4), (2, 8)), jnp.float32),
        "obs_cells": draw_obs_cells(jax.random.fold_in(keys[6], 71), 0),
        "obs_values": scatter_about(keys[4], (SURVEYS, OBS), 1.0, 6.0, ((1, 8),), jnp.float32),
        "seismic_mask": plant((jax.random.randint(keys[5], (SURVEYS, NCELLS // 128), 0, 4) < 3).astype(jnp.int32), jax.random.fold_in(keys[5], 1), 0, 1),
    }


def reference(prior, samples, noise, obs_cells, obs_values, seismic_mask):
    ncell = prior.shape[1]
    precision_field = jnp.zeros((ncell,), jnp.float32)
    target_field = jnp.zeros((ncell,), jnp.float32)
    for survey in range(obs_cells.shape[0]):
        where = obs_cells[survey].astype(jnp.int32)
        flags = seismic_mask[survey].astype(jnp.float32)
        weight = flags[where // 128]
        precision_field = precision_field.at[where].add(weight)
        target_field = target_field.at[where].add(weight * obs_values[survey])
    prior_sq = lax.optimization_barrier(jnp.sum(prior * prior, axis=1))
    state = samples
    for step in range(STEPS):
        time_now = 0.6 - 0.1 * step
        alpha = 1.0 - 0.95 * time_now
        beta2 = time_now
        drift = -0.95 / alpha
        diffusion = 1.0 - 2.0 * drift * beta2
        cross = lax.dot_general(state, prior, (((1,), (1,)), ((), ())), precision=lax.Precision.HIGHEST, preferred_element_type=jnp.float32)
        dist = alpha * alpha * prior_sq[None, :] - 2.0 * alpha * cross
        weights = jax.nn.softmax(-dist / (2.0 * beta2 * math.sqrt(ncell)), axis=1)
        mean = jnp.dot(weights, prior, precision=lax.Precision.HIGHEST, preferred_element_type=jnp.float32)
        score = (alpha * mean - state) / beta2 - (1.0 - time_now) * (precision_field[None, :] * state - target_field[None, :])
        state = state - 0.1 * (drift * state - diffusion * score) + math.sqrt(0.1 * diffusion) * noise[step]
    return state
```

```python
import functools
import math

import jax
import jax.numpy as jnp
from jax import lax
from jax.experimental import pallas as pl
from jax.experimental.pallas import tpu as pltpu
from jax.sharding import PartitionSpec as P

STEPS = 2
LANES = 128
CHUNKS = 8
OBS_CHUNK = 512
MESH = pl.DeviceIdType.MESH
NT = (((1,), (1,)), ((), ()))


def constants(step):
    time_now = 0.6 - 0.1 * step
    alpha = 1.0 - 0.95 * time_now
    drift = -0.95 / alpha
    diffusion = 1.0 - 2.0 * drift * time_now
    keep = 1.0 - 0.1 * drift - 0.1 * diffusion / time_now
    obs = 0.1 * diffusion * (1.0 - time_now)
    pull = 0.1 * diffusion * alpha / time_now
    spread = math.sqrt(0.1 * diffusion)
    return time_now, alpha, keep, obs, pull, spread


def split(x):
    high = x.astype(jnp.bfloat16)
    low = (x - high.astype(jnp.float32)).astype(jnp.bfloat16)
    return high, low


def softmax_rows(logits):
    top = jnp.max(logits, axis=1, keepdims=True)
    e = jnp.exp(logits - top)
    return e / jnp.sum(e, axis=1, keepdims=True)


def kernel(
    groups,
    shards,
    prior_ref,
    samples_ref,
    noise_ref,
    cells_ref,
    values_ref,
    mask_ref,
    out_ref,
    gath,
    samples_v,
    noise_v,
    split_sy,
    split_p,
    base_v,
    scale_v,
    result_v,
    field_v,
    acc,
    inbox,
    outbox,
    local_sem,
    out_sem,
    send_sem,
    recv_sem,
    red_send,
    red_recv,
):
    me = lax.axis_index("member")
    shard = lax.axis_index("cell")
    rows, cells = prior_ref.shape
    ens = rows * groups
    width = cells // CHUNKS
    ncell = cells * shards
    rounds = shards.bit_length() - 1

    def span(c):
        return pl.ds(pl.multiple_of(c * width, width), width)

    def hop(way, origin, c, own=False):
        target = me + 1 if way == 0 else me - 1
        block = gath.at[origin, :, span(c)]
        return pltpu.make_async_remote_copy(
            src_ref=prior_ref.at[:, span(c)] if own else block,
            dst_ref=block,
            send_sem=send_sem.at[way, origin, c],
            recv_sem=recv_sem.at[origin, c],
            device_id={"member": target},
            device_id_type=MESH,
        )

    def partner(r):
        bit = 1 << r
        return shard + bit * (1 - 2 * ((shard // bit) % 2))

    loads = [
        pltpu.make_async_copy(prior_ref, gath.at[me], local_sem.at[0]),
        pltpu.make_async_copy(samples_ref, samples_v, local_sem.at[1]),
        pltpu.make_async_copy(noise_ref, noise_v, local_sem.at[2]),
    ]
    for load in loads:
        load.start()

    barrier = pltpu.get_barrier_semaphore()

    @pl.when(me > 0)
    def _():
        pl.semaphore_signal(barrier, inc=1, device_id={"member": me - 1}, device_id_type=MESH)

    @pl.when(me < groups - 1)
    def _():
        pl.semaphore_signal(barrier, inc=1, device_id={"member": me + 1}, device_id_type=MESH)

    for r in range(rounds):
        pl.semaphore_signal(barrier, inc=1, device_id={"cell": partner(r)}, device_id_type=MESH)
    inner = (me > 0) & (me < groups - 1)

    @pl.when(inner)
    def _():
        pl.semaphore_wait(barrier, rounds + 2)

    @pl.when(jnp.logical_not(inner))
    def _():
        pl.semaphore_wait(barrier, rounds + 1)

    def send_own(c, _):
        @pl.when(me < groups - 1)
        def _():
            hop(0, me, c, own=True).start()

        @pl.when(me > 0)
        def _():
            hop(1, me, c, own=True).start()

        return 0

    lax.fori_loop(0, CHUNKS, send_own, 0)

    blocks = cells // LANES
    count_obs = cells_ref.shape[1]
    piece = min(OBS_CHUNK, count_obs)
    eye = lax.broadcasted_iota(jnp.int32, (blocks, blocks), 0) == lax.broadcasted_iota(
        jnp.int32, (blocks, blocks), 1
    )
    field_v[...] = jnp.zeros_like(field_v)
    for survey in range(cells_ref.shape[0]):

        def gather_obs(o, total, survey=survey):
            at = pl.ds(pl.multiple_of(o * piece, piece), piece)
            where = cells_ref[survey : survey + 1, at] - shard * cells
            values = values_ref[survey : survey + 1, at]
            block_of = where // LANES
            lane_of = where - block_of * LANES
            first = (
                lax.broadcasted_iota(jnp.int32, (blocks, piece), 0) == block_of
            )
            second = lax.broadcasted_iota(jnp.int32, (LANES, piece), 0) == lane_of
            one = values.astype(jnp.bfloat16).astype(jnp.float32)
            two = (values - one).astype(jnp.bfloat16).astype(jnp.float32)
            three = values - one - two
            left = jnp.where(first, 1.0, 0.0).astype(jnp.bfloat16)
            right = jnp.concatenate(
                [
                    jnp.where(second, part, 0.0).astype(jnp.bfloat16)
                    for part in (jnp.ones_like(values), one, two, three)
                ],
                axis=0,
            )
            return total + lax.dot_general(left, right, NT, preferred_element_type=jnp.float32)

        total = lax.fori_loop(
            0, count_obs // piece, gather_obs, jnp.zeros((blocks, 4 * LANES), jnp.float32)
        )
        flags = mask_ref[survey : survey + 1, :].astype(jnp.float32)
        column = jnp.sum(jnp.where(eye, flags, 0.0), axis=1, keepdims=True)
        field_v[0] += column * total[:, :LANES]
        field_v[1] += column * (
            total[:, LANES : 2 * LANES]
            + total[:, 2 * LANES : 3 * LANES]
            + total[:, 3 * LANES : 4 * LANES]
        )

    loads[1].wait()
    loads[2].wait()
    _, _, keep0, obs0, pull0, spread0 = constants(0)
    _, _, keep1, obs1, pull1, spread1 = constants(1)

    def prepare(h, _):
        at = pl.ds(pl.multiple_of(h * LANES, LANES), LANES)
        precision = field_v[0, pl.ds(h, 1), :]
        target = field_v[1, pl.ds(h, 1), :]
        state = samples_v[:, at]
        moved = (keep0 - obs0 * precision) * state + obs0 * target + spread0 * noise_v[0, :, at]
        factor = keep1 - obs1 * precision
        base_v[:, at] = factor * moved + obs1 * target + spread1 * noise_v[1, :, at]
        scale_v[:, at] = jnp.broadcast_to(pull0 * factor, (rows, LANES))
        high, low = split(jnp.concatenate([state, moved], axis=0))
        split_sy[: 2 * rows, at] = high
        split_sy[2 * rows :, at] = low
        return 0

    lax.fori_loop(0, blocks, prepare, 0)
    loads[0].wait()
    acc[...] = jnp.zeros_like(acc)

    def products(c):
        at = span(c)
        high, low = split(gath[:, :, at].reshape(ens, width))
        split_p[:ens, at] = high
        split_p[ens:, at] = low
        right = jnp.concatenate([high, low], axis=0)
        left = jnp.concatenate([split_sy[:, at], right], axis=0)
        acc[...] += lax.dot_general(left, right, NT, preferred_element_type=jnp.float32)

    for d in range(1, groups):

        def relay(c, _, d=d):
            @pl.when(me - d >= 0)
            def _():
                hop(1, me - d, c).wait_recv()

                @pl.when(me < groups - 1)
                def _():
                    hop(0, me - d, c).start()

            @pl.when(me + d < groups)
            def _():
                hop(0, me + d, c).wait_recv()

                @pl.when(me > 0)
                def _():
                    hop(1, me + d, c).start()

            if d == groups - 1:
                products(c)
            return 0

        lax.fori_loop(0, CHUNKS, relay, 0)

    whole = acc[...]
    four = 4 * rows
    sy = whole[: 2 * rows] + whole[2 * rows : four]
    gram = whole[four : four + ens] + whole[four + ens :]
    part = jnp.concatenate([sy, gram], axis=0)
    part = part[:, :ens] + part[:, ens:]
    half = part.shape[0] // 2
    part = jnp.concatenate([part[:half], part[half:]], axis=1)
    for r in range(rounds):
        outbox[r] = part
        swap = pltpu.make_async_remote_copy(
            src_ref=outbox.at[r],
            dst_ref=inbox.at[r],
            send_sem=red_send.at[r],
            recv_sem=red_recv.at[r],
            device_id={"cell": partner(r)},
            device_id_type=MESH,
        )
        swap.start()
        swap.wait()
        part = part + inbox[r]
    part = jnp.concatenate([part[:, :ens], part[:, ens:]], axis=0)
    cross0 = part[:rows]
    cross1 = part[rows : 2 * rows]
    gram = part[2 * rows :]
    diagonal = lax.broadcasted_iota(jnp.int32, (ens, ens), 0) == lax.broadcasted_iota(
        jnp.int32, (ens, ens), 1
    )
    prior_sq = jnp.sum(jnp.where(diagonal, gram, 0.0), axis=0, keepdims=True)

    def weigh(step, cross):
        time_now, alpha = constants(step)[:2]
        dist = alpha * alpha * prior_sq - 2.0 * alpha * cross
        return softmax_rows(-dist / (2.0 * time_now * math.sqrt(ncell)))

    weights0 = weigh(0, cross0)
    cross1 = cross1 + pull0 * jnp.dot(
        weights0, gram, precision=lax.Precision.HIGHEST, preferred_element_type=jnp.float32
    )
    weights1 = weigh(1, cross1)
    high, low = split(jnp.concatenate([weights0, weights1], axis=0))
    both = jnp.concatenate([high, low], axis=0)
    both = jnp.concatenate([both, both], axis=1)

    def store(c):
        return pltpu.make_async_copy(
            result_v.at[:, span(c)], out_ref.at[:, span(c)], out_sem.at[c]
        )

    def finish(c, _):
        at = span(c)
        mean = jnp.dot(both, split_p[:, at], preferred_element_type=jnp.float32)
        mean = mean[: 2 * rows] + mean[2 * rows :]
        result_v[:, at] = base_v[:, at] + scale_v[:, at] * mean[:rows] + pull1 * mean[rows:]
        store(c).start()
        return 0

    lax.fori_loop(0, CHUNKS, finish, 0)

    def drain(c, _):
        store(c).wait()
        for origin in range(groups):

            @pl.when((origin <= me) & (me < groups - 1))
            def _():
                hop(0, origin, c).wait_send()

            @pl.when((origin >= me) & (me > 0))
            def _():
                hop(1, origin, c).wait_send()

        return 0

    lax.fori_loop(0, CHUNKS, drain, 0)


def per_device(prior, samples, noise, obs_cells, obs_values, seismic_mask):
    rows, cells = prior.shape
    groups = lax.axis_size("member")
    shards = lax.axis_size("cell")
    ens = rows * groups
    rounds = shards.bit_length() - 1
    half = (2 * rows + ens) // 2
    hbm = pl.BlockSpec(memory_space=pl.ANY)
    vmem = pl.BlockSpec(memory_space=pltpu.VMEM)
    f32 = jnp.float32
    return pl.pallas_call(
        functools.partial(kernel, groups, shards),
        out_shape=jax.ShapeDtypeStruct((rows, cells), f32),
        in_specs=[hbm, hbm, hbm, vmem, vmem, vmem],
        out_specs=hbm,
        scratch_shapes=[
            pltpu.VMEM((groups, rows, cells), f32),
            pltpu.VMEM((rows, cells), f32),
            pltpu.VMEM((STEPS, rows, cells), f32),
            pltpu.VMEM((4 * rows, cells), jnp.bfloat16),
            pltpu.VMEM((2 * ens, cells), jnp.bfloat16),
            pltpu.VMEM((rows, cells), f32),
            pltpu.VMEM((rows, cells), f32),
            pltpu.VMEM((rows, cells), f32),
            pltpu.VMEM((2, cells // LANES, LANES), f32),
            pltpu.VMEM((4 * rows + 2 * ens, 2 * ens), f32),
            pltpu.VMEM((rounds, half, 2 * ens), f32),
            pltpu.VMEM((rounds, half, 2 * ens), f32),
            pltpu.SemaphoreType.DMA((3,)),
            pltpu.SemaphoreType.DMA((CHUNKS,)),
            pltpu.SemaphoreType.DMA((2, groups, CHUNKS)),
            pltpu.SemaphoreType.DMA((groups, CHUNKS)),
            pltpu.SemaphoreType.DMA((rounds,)),
            pltpu.SemaphoreType.DMA((rounds,)),
        ],
        compiler_params=pltpu.CompilerParams(
            collective_id=0, has_side_effects=True, vmem_limit_bytes=48 * 1024 * 1024
        ),
    )(prior, samples, noise, obs_cells, obs_values, seismic_mask)


def solution(mesh):
    in_specs = (
        P("member", "cell"),
        P("member", "cell"),
        P(None, "member", "cell"),
        P(None, "cell"),
        P(None, "cell"),
        P(None, "cell"),
    )
    out_specs = P("member", "cell")
    return jax.shard_map(
        per_device, mesh=mesh, in_specs=in_specs, out_specs=out_specs, check_vma=False
    )
```

```python
import functools
import math

import jax
import jax.numpy as jnp
from jax import lax
from jax.experimental import pallas as pl
from jax.experimental.pallas import tpu as pltpu
from jax.sharding import PartitionSpec as P

STEPS = 2
LANES = 128
CHUNKS = 16
GUEST = 5
OBS_CHUNK = 512
MESH = pl.DeviceIdType.MESH
NT = (((1,), (1,)), ((), ()))


def constants(step):
    time_now = 0.6 - 0.1 * step
    alpha = 1.0 - 0.95 * time_now
    drift = -0.95 / alpha
    diffusion = 1.0 - 2.0 * drift * time_now
    keep = 1.0 - 0.1 * drift - 0.1 * diffusion / time_now
    obs = 0.1 * diffusion * (1.0 - time_now)
    pull = 0.1 * diffusion * alpha / time_now
    spread = math.sqrt(0.1 * diffusion)
    return time_now, alpha, keep, obs, pull, spread


def split(x):
    high = x.astype(jnp.bfloat16)
    low = (x - high.astype(jnp.float32)).astype(jnp.bfloat16)
    return high, low


def softmax_rows(logits):
    top = jnp.max(logits, axis=1, keepdims=True)
    e = jnp.exp(logits - top)
    return e / jnp.sum(e, axis=1, keepdims=True)


def kernel(
    groups,
    shards,
    prior_ref,
    samples_ref,
    noise_ref,
    cells_ref,
    values_ref,
    mask_ref,
    out_ref,
    cells_v,
    values_v,
    mask_v,
    gath,
    samples_v,
    noise_v,
    split_sy,
    split_p,
    base_v,
    scale_v,
    result_v,
    field_v,
    acc,
    inbox,
    outbox,
    local_sem,
    out_sem,
    send_sem,
    recv_sem,
    red_send,
    red_recv,
    guest_in,
    guest_sy,
    guest_out,
    guest_mean,
    guest_acc,
    guest_part,
    guest_weights,
    guest_send,
    guest_recv,
    mean_send,
    mean_recv,
):
    me = lax.axis_index("member")
    shard = lax.axis_index("cell")
    rows, cells = prior_ref.shape
    ens = rows * groups
    width = cells // CHUNKS
    ncell = cells * shards
    rounds = shards.bit_length() - 1
    low = 1 - (2 * me) // groups
    end = (me == 0) | (me == groups - 1)
    helper = (me == 1) | (me == groups - 2)
    outward = 1 - 2 * low
    held = GUEST * width

    def span(c):
        return pl.ds(pl.multiple_of(c * width, width), width)

    def hop(way, origin, c, own=False):
        target = me + 1 if way == 0 else me - 1
        block = gath.at[origin, :, span(c)]
        return pltpu.make_async_remote_copy(
            src_ref=prior_ref.at[:, span(c)] if own else block,
            dst_ref=block,
            send_sem=send_sem.at[way, origin, c],
            recv_sem=recv_sem.at[origin, c],
            device_id={"member": target},
            device_id_type=MESH,
        )

    def to_helper(i):
        source = samples_ref if i == 0 else noise_ref.at[0]
        return pltpu.make_async_remote_copy(
            src_ref=source.at[:, :held],
            dst_ref=guest_in.at[i],
            send_sem=guest_send.at[i],
            recv_sem=guest_recv.at[i],
            device_id={"member": me - outward},
            device_id_type=MESH,
        )

    def part_to_end(way=1):
        return pltpu.make_async_remote_copy(
            src_ref=guest_part.at[0],
            dst_ref=guest_part.at[1],
            send_sem=guest_send.at[2],
            recv_sem=guest_recv.at[2],
            device_id={"member": me + way * outward},
            device_id_type=MESH,
        )

    def weights_to_helper():
        return pltpu.make_async_remote_copy(
            src_ref=guest_weights.at[0],
            dst_ref=guest_weights.at[1],
            send_sem=guest_send.at[3],
            recv_sem=guest_recv.at[3],
            device_id={"member": me - outward},
            device_id_type=MESH,
        )

    def mean_to_end(c, way=1):
        return pltpu.make_async_remote_copy(
            src_ref=guest_out.at[:, span(c)],
            dst_ref=guest_mean.at[:, span(c)],
            send_sem=mean_send.at[c],
            recv_sem=mean_recv.at[c],
            device_id={"member": me + way * outward},
            device_id_type=MESH,
        )

    def partner(r):
        bit = 1 << r
        return shard + bit * (1 - 2 * ((shard // bit) % 2))

    loads = [
        pltpu.make_async_copy(prior_ref, gath.at[me], local_sem.at[0]),
        pltpu.make_async_copy(samples_ref, samples_v, local_sem.at[1]),
        pltpu.make_async_copy(noise_ref, noise_v, local_sem.at[2]),
        pltpu.make_async_copy(cells_ref, cells_v, local_sem.at[3]),
        pltpu.make_async_copy(values_ref, values_v, local_sem.at[4]),
        pltpu.make_async_copy(mask_ref, mask_v, local_sem.at[5]),
    ]
    for load in loads:
        load.start()

    barrier = pltpu.get_barrier_semaphore()

    @pl.when(me > 0)
    def _():
        pl.semaphore_signal(barrier, inc=1, device_id={"member": me - 1}, device_id_type=MESH)

    @pl.when(me < groups - 1)
    def _():
        pl.semaphore_signal(barrier, inc=1, device_id={"member": me + 1}, device_id_type=MESH)

    for r in range(rounds):
        pl.semaphore_signal(barrier, inc=1, device_id={"cell": partner(r)}, device_id_type=MESH)
    inner = (me > 0) & (me < groups - 1)

    @pl.when(inner)
    def _():
        pl.semaphore_wait(barrier, rounds + 2)

    @pl.when(jnp.logical_not(inner))
    def _():
        pl.semaphore_wait(barrier, rounds + 1)

    @pl.when(end)
    def _():
        to_helper(0).start()
        to_helper(1).start()

    def goes(way, c_held):
        rim = 1 if c_held else 0
        return me < groups - 1 - rim if way == 0 else me > rim

    def send_own(c, _, c_held):
        for way in range(2):

            @pl.when(goes(way, c_held))
            def _(way=way):
                hop(way, me, c, own=True).start()

        return 0

    lax.fori_loop(0, GUEST, functools.partial(send_own, c_held=True), 0)
    lax.fori_loop(GUEST, CHUNKS, functools.partial(send_own, c_held=False), 0)
    for load in loads[3:]:
        load.wait()

    blocks = cells // LANES
    count_obs = cells_ref.shape[1]
    piece = min(OBS_CHUNK, count_obs)
    eye = lax.broadcasted_iota(jnp.int32, (blocks, blocks), 0) == lax.broadcasted_iota(
        jnp.int32, (blocks, blocks), 1
    )
    field_v[...] = jnp.zeros_like(field_v)
    for survey in range(cells_ref.shape[0]):

        def gather_obs(o, total, survey=survey):
            at = pl.ds(pl.multiple_of(o * piece, piece), piece)
            where = cells_v[survey : survey + 1, at] - shard * cells
            values = values_v[survey : survey + 1, at]
            block_of = where // LANES
            lane_of = where - block_of * LANES
            first = (
                lax.broadcasted_iota(jnp.int32, (blocks, piece), 0) == block_of
            )
            second = lax.broadcasted_iota(jnp.int32, (LANES, piece), 0) == lane_of
            one = values.astype(jnp.bfloat16).astype(jnp.float32)
            two = (values - one).astype(jnp.bfloat16).astype(jnp.float32)
            three = values - one - two
            left = jnp.where(first, 1.0, 0.0).astype(jnp.bfloat16)
            right = jnp.concatenate(
                [
                    jnp.where(second, part, 0.0).astype(jnp.bfloat16)
                    for part in (jnp.ones_like(values), one, two, three)
                ],
                axis=0,
            )
            return total + lax.dot_general(left, right, NT, preferred_element_type=jnp.float32)

        total = lax.fori_loop(
            0, count_obs // piece, gather_obs, jnp.zeros((blocks, 4 * LANES), jnp.float32)
        )
        flags = mask_v[survey : survey + 1, :].astype(jnp.float32)
        column = jnp.sum(jnp.where(eye, flags, 0.0), axis=1, keepdims=True)
        field_v[0] += column * total[:, :LANES]
        field_v[1] += column * (
            total[:, LANES : 2 * LANES]
            + total[:, 2 * LANES : 3 * LANES]
            + total[:, 3 * LANES : 4 * LANES]
        )

    loads[1].wait()
    loads[2].wait()
    _, _, keep0, obs0, pull0, spread0 = constants(0)
    _, _, keep1, obs1, pull1, spread1 = constants(1)

    def advance(state, fresh, precision, target):
        return (keep0 - obs0 * precision) * state + obs0 * target + spread0 * fresh

    def prepare(h, _):
        at = pl.ds(pl.multiple_of(h * LANES, LANES), LANES)
        precision = field_v[0, pl.ds(h, 1), :]
        target = field_v[1, pl.ds(h, 1), :]
        state = samples_v[:, at]
        moved = advance(state, noise_v[0, :, at], precision, target)
        factor = keep1 - obs1 * precision
        base_v[:, at] = factor * moved + obs1 * target + spread1 * noise_v[1, :, at]
        scale_v[:, at] = jnp.broadcast_to(pull0 * factor, (rows, LANES))
        high, low = split(jnp.concatenate([state, moved], axis=0))
        split_sy[: 2 * rows, at] = high
        split_sy[2 * rows :, at] = low
        return 0

    def prepare_guest(h, _):
        at = pl.ds(pl.multiple_of(h * LANES, LANES), LANES)
        precision = field_v[0, pl.ds(h, 1), :]
        target = field_v[1, pl.ds(h, 1), :]
        state = guest_in[0, :, at]
        moved = advance(state, guest_in[1, :, at], precision, target)
        high, low = split(jnp.concatenate([state, moved], axis=0))
        guest_sy[: 2 * rows, at] = high
        guest_sy[2 * rows :, at] = low
        return 0

    lax.fori_loop(0, blocks, prepare, 0)
    loads[0].wait()
    acc[...] = jnp.zeros_like(acc)

    four = 4 * rows

    def products(c, guest):
        at = span(c)
        high, low = split(gath[:, :, at].reshape(ens, width))
        split_p[:ens, at] = high
        split_p[ens:, at] = low
        right = jnp.concatenate([high, low], axis=0)
        first = [split_sy[:, at], guest_sy[:, at]] if guest else [split_sy[:, at]]
        left = jnp.concatenate(first + [right], axis=0)
        total = guest_acc if guest else acc
        total[...] += lax.dot_general(left, right, NT, preferred_element_type=jnp.float32)

    def fold(sy, gram):
        part = jnp.concatenate(
            [sy[: 2 * rows] + sy[2 * rows :], gram[:ens] + gram[ens:]], axis=0
        )
        part = part[:, :ens] + part[:, ens:]
        half = part.shape[0] // 2
        return jnp.concatenate([part[:half], part[half:]], axis=1)

    def relay(c, _, d, c_held):
        comes = (me < groups - 1, me > 0) if c_held else (True, True)

        @pl.when((me - d >= 0) & comes[0])
        def _():
            hop(1, me - d, c).wait_recv()

            @pl.when(goes(0, c_held))
            def _():
                hop(0, me - d, c).start()

        @pl.when((me + d < groups) & comes[1])
        def _():
            hop(0, me + d, c).wait_recv()

            @pl.when(goes(1, c_held))
            def _():
                hop(1, me + d, c).start()

        if 2 * d >= groups and not (c_held and d == groups - 1):

            @pl.when((me == d) | (me == groups - 1 - d))
            def _():
                products(c, c_held and d == groups - 2)

        return 0

    for d in range(1, groups):
        if d == groups - 2:

            @pl.when(helper)
            def _():
                to_helper(0).wait_recv()
                to_helper(1).wait_recv()
                guest_acc[...] = jnp.zeros_like(guest_acc)
                lax.fori_loop(0, held // LANES, prepare_guest, 0)

        lax.fori_loop(0, GUEST, functools.partial(relay, d=d, c_held=True), 0)
        if d == groups - 2:

            @pl.when(helper)
            def _():
                acc[:four] = guest_acc[:four]
                acc[four:] = guest_acc[2 * four :]
                guest_part[0] = fold(guest_acc[four : 2 * four], guest_acc[2 * four :])
                part_to_end().start()

        lax.fori_loop(GUEST, CHUNKS, functools.partial(relay, d=d, c_held=False), 0)

    outbox[0] = fold(acc[:four], acc[four:])

    @pl.when(end)
    def _():
        part_to_end(-1).wait_recv()
        outbox[0] += guest_part[1]

    part = outbox[0]
    for r in range(rounds):
        if r > 0:
            outbox[r] = part
        swap = pltpu.make_async_remote_copy(
            src_ref=outbox.at[r],
            dst_ref=inbox.at[r],
            send_sem=red_send.at[r],
            recv_sem=red_recv.at[r],
            device_id={"cell": partner(r)},
            device_id_type=MESH,
        )
        swap.start()
        swap.wait()
        part = part + inbox[r]
    part = jnp.concatenate([part[:, :ens], part[:, ens:]], axis=0)
    cross0 = part[:rows]
    cross1 = part[rows : 2 * rows]
    gram = part[2 * rows :]
    diagonal = lax.broadcasted_iota(jnp.int32, (ens, ens), 0) == lax.broadcasted_iota(
        jnp.int32, (ens, ens), 1
    )
    prior_sq = jnp.sum(jnp.where(diagonal, gram, 0.0), axis=0, keepdims=True)

    def weigh(step, cross):
        time_now, alpha = constants(step)[:2]
        dist = alpha * alpha * prior_sq - 2.0 * alpha * cross
        return softmax_rows(-dist / (2.0 * time_now * math.sqrt(ncell)))

    weights0 = weigh(0, cross0)
    cross1 = cross1 + pull0 * jnp.dot(
        weights0, gram, precision=lax.Precision.HIGHEST, preferred_element_type=jnp.float32
    )
    weights1 = weigh(1, cross1)
    weights = jnp.concatenate([weights0, weights1], axis=0)

    @pl.when(end)
    def _():
        guest_weights[0] = jnp.concatenate([weights, weights], axis=1)
        weights_to_helper().start()

    def stack(high, low):
        both = jnp.concatenate([high, low], axis=0)
        return both if both.shape[1] == 2 * ens else jnp.concatenate([both, both], axis=1)

    def means(both, c):
        at = span(c)
        mean = jnp.dot(both, split_p[:, at], preferred_element_type=jnp.float32)
        mean = mean[: 2 * rows] + mean[2 * rows :]
        return scale_v[:, at] * mean[:rows] + pull1 * mean[rows:]

    @pl.when(helper)
    def _():
        weights_to_helper().wait_recv()
        guest_both = stack(*split(guest_weights[1]))

        def serve(c, _):
            guest_out[:, span(c)] = means(guest_both, c)
            mean_to_end(c).start()
            return 0

        lax.fori_loop(0, GUEST, serve, 0)

    both = stack(*split(weights))

    def store(c):
        return pltpu.make_async_copy(
            result_v.at[:, span(c)], out_ref.at[:, span(c)], out_sem.at[c]
        )

    def finish(c, _):
        at = span(c)
        result_v[:, at] = base_v[:, at] + means(both, c)
        store(c).start()
        return 0

    def finish_held(c, _):
        at = span(c)
        mean_to_end(c, -1).wait_recv()
        result_v[:, at] = base_v[:, at] + guest_mean[:, at]
        store(c).start()
        return 0

    lax.fori_loop(GUEST, CHUNKS, finish, 0)

    @pl.when(end)
    def _():
        lax.fori_loop(0, GUEST, finish_held, 0)
        to_helper(0).wait_send()
        to_helper(1).wait_send()
        weights_to_helper().wait_send()

    @pl.when(jnp.logical_not(end))
    def _():
        lax.fori_loop(0, GUEST, finish, 0)

    @pl.when(helper)
    def _():
        part_to_end().wait_send()

    def drain(c, _, c_held):
        store(c).wait()
        for origin in range(groups):

            @pl.when((origin <= me) & goes(0, c_held))
            def _(origin=origin):
                hop(0, origin, c).wait_send()

            @pl.when((origin >= me) & goes(1, c_held))
            def _(origin=origin):
                hop(1, origin, c).wait_send()

        if c_held:

            @pl.when(helper)
            def _():
                mean_to_end(c).wait_send()

        return 0

    lax.fori_loop(0, GUEST, functools.partial(drain, c_held=True), 0)
    lax.fori_loop(GUEST, CHUNKS, functools.partial(drain, c_held=False), 0)


def per_device(prior, samples, noise, obs_cells, obs_values, seismic_mask):
    rows, cells = prior.shape
    groups = lax.axis_size("member")
    shards = lax.axis_size("cell")
    ens = rows * groups
    rounds = shards.bit_length() - 1
    half = (2 * rows + ens) // 2
    held = GUEST * (cells // CHUNKS)
    hbm = pl.BlockSpec(memory_space=pl.ANY)
    f32 = jnp.float32
    return pl.pallas_call(
        functools.partial(kernel, groups, shards),
        out_shape=jax.ShapeDtypeStruct((rows, cells), f32),
        in_specs=[hbm] * 6,
        out_specs=hbm,
        scratch_shapes=[
            pltpu.VMEM(obs_cells.shape, jnp.int32),
            pltpu.VMEM(obs_values.shape, f32),
            pltpu.VMEM(seismic_mask.shape, jnp.int32),
            pltpu.VMEM((groups, rows, cells), f32),
            pltpu.VMEM((rows, cells), f32),
            pltpu.VMEM((STEPS, rows, cells), f32),
            pltpu.VMEM((4 * rows, cells), jnp.bfloat16),
            pltpu.VMEM((2 * ens, cells), jnp.bfloat16),
            pltpu.VMEM((rows, cells), f32),
            pltpu.VMEM((rows, cells), f32),
            pltpu.VMEM((rows, cells), f32),
            pltpu.VMEM((2, cells // LANES, LANES), f32),
            pltpu.VMEM((4 * rows + 2 * ens, 2 * ens), f32),
            pltpu.VMEM((rounds, half, 2 * ens), f32),
            pltpu.VMEM((rounds, half, 2 * ens), f32),
            pltpu.SemaphoreType.DMA((6,)),
            pltpu.SemaphoreType.DMA((CHUNKS,)),
            pltpu.SemaphoreType.DMA((2, groups, CHUNKS)),
            pltpu.SemaphoreType.DMA((groups, CHUNKS)),
            pltpu.SemaphoreType.DMA((rounds,)),
            pltpu.SemaphoreType.DMA((rounds,)),
            pltpu.VMEM((2, rows, held), f32),
            pltpu.VMEM((4 * rows, held), jnp.bfloat16),
            pltpu.VMEM((rows, held), f32),
            pltpu.VMEM((rows, held), f32),
            pltpu.VMEM((8 * rows + 2 * ens, 2 * ens), f32),
            pltpu.VMEM((2, half, 2 * ens), f32),
            pltpu.VMEM((2, 2 * rows, 2 * ens), f32),
            pltpu.SemaphoreType.DMA((4,)),
            pltpu.SemaphoreType.DMA((4,)),
            pltpu.SemaphoreType.DMA((GUEST,)),
            pltpu.SemaphoreType.DMA((GUEST,)),
        ],
        compiler_params=pltpu.CompilerParams(
            collective_id=0, has_side_effects=True, vmem_limit_bytes=60 * 1024 * 1024
        ),
    )(prior, samples, noise, obs_cells, obs_values, seismic_mask)


def solution(mesh):
    in_specs = (
        P("member", "cell"),
        P("member", "cell"),
        P(None, "member", "cell"),
        P(None, "cell"),
        P(None, "cell"),
        P(None, "cell"),
    )
    out_specs = P("member", "cell")
    return jax.shard_map(
        per_device, mesh=mesh, in_specs=in_specs, out_specs=out_specs, check_vma=False
    )
```

```python
import functools
import math

import jax
import jax.numpy as jnp
from jax import lax
from jax.experimental import pallas as pl
from jax.experimental.pallas import tpu as pltpu
from jax.sharding import PartitionSpec as P

STEPS = 2
LANES = 128
CHUNKS = 16
THIRD = 3
GUEST = CHUNKS // THIRD
LAG = 2
AHEAD = 8
OBS_CHUNK = 512
MESH = pl.DeviceIdType.MESH
NT = (((1,), (1,)), ((), ()))


def constants(step):
    time_now = 0.6 - 0.1 * step
    alpha = 1.0 - 0.95 * time_now
    drift = -0.95 / alpha
    diffusion = 1.0 - 2.0 * drift * time_now
    keep = 1.0 - 0.1 * drift - 0.1 * diffusion / time_now
    obs = 0.1 * diffusion * (1.0 - time_now)
    pull = 0.1 * diffusion * alpha / time_now
    spread = math.sqrt(0.1 * diffusion)
    return time_now, alpha, keep, obs, pull, spread


def split(x):
    high = x.astype(jnp.bfloat16)
    low = (x - high.astype(jnp.float32)).astype(jnp.bfloat16)
    return high, low


def softmax_rows(logits):
    top = jnp.max(logits, axis=1, keepdims=True)
    e = jnp.exp(logits - top)
    return e / jnp.sum(e, axis=1, keepdims=True)


def kernel(
    groups,
    shards,
    prior_ref,
    samples_ref,
    noise_ref,
    cells_ref,
    values_ref,
    mask_ref,
    out_ref,
    cells_v,
    values_v,
    mask_v,
    gath,
    samples_v,
    noise_v,
    split_sy,
    split_p,
    base_v,
    scale_v,
    result_v,
    field_v,
    acc,
    inbox,
    outbox,
    local_sem,
    out_sem,
    send_sem,
    recv_sem,
    red_send,
    red_recv,
    guest_in,
    guest_sy,
    guest_out,
    guest_mean,
    guest_acc,
    guest_part,
    guest_weights,
    in_send,
    in_recv,
    guest_send,
    guest_recv,
    mean_send,
    mean_recv,
):
    me = lax.axis_index("member")
    shard = lax.axis_index("cell")
    rows, cells = prior_ref.shape
    ens = rows * groups
    width = cells // CHUNKS
    ncell = cells * shards
    rounds = shards.bit_length() - 1
    low = 1 - (2 * me) // groups
    end = (me == 0) | (me == groups - 1)
    helper = (me == 1) | (me == groups - 2)
    outward = 1 - 2 * low
    furthest = me + low * (groups - 1 - 2 * me)
    steps = CHUNKS + LAG * (groups - 1)

    def span(c):
        return pl.ds(pl.multiple_of(c * width, width), width)

    def hop(way, origin, c, own=False):
        target = me + 1 if way == 0 else me - 1
        block = gath.at[origin, :, span(c)]
        return pltpu.make_async_remote_copy(
            src_ref=prior_ref.at[:, span(c)] if own else block,
            dst_ref=block,
            send_sem=send_sem.at[way, origin, c],
            recv_sem=recv_sem.at[origin, c],
            device_id={"member": target},
            device_id_type=MESH,
        )

    def left_out(c):
        return c % THIRD == 1

    def to_helper(i, g):
        source = samples_ref if i == 0 else noise_ref.at[0]
        return pltpu.make_async_remote_copy(
            src_ref=source.at[:, span(THIRD * g + 1)],
            dst_ref=guest_in.at[i, :, span(g)],
            send_sem=in_send.at[i, g],
            recv_sem=in_recv.at[i, g],
            device_id={"member": me - outward},
            device_id_type=MESH,
        )

    def part_to_end(way=1):
        return pltpu.make_async_remote_copy(
            src_ref=guest_part.at[0],
            dst_ref=guest_part.at[1],
            send_sem=guest_send.at[0],
            recv_sem=guest_recv.at[0],
            device_id={"member": me + way * outward},
            device_id_type=MESH,
        )

    def weights_to_helper():
        return pltpu.make_async_remote_copy(
            src_ref=guest_weights.at[0],
            dst_ref=guest_weights.at[1],
            send_sem=guest_send.at[1],
            recv_sem=guest_recv.at[1],
            device_id={"member": me - outward},
            device_id_type=MESH,
        )

    def mean_to_end(g, way=1):
        return pltpu.make_async_remote_copy(
            src_ref=guest_out.at[:, span(g)],
            dst_ref=guest_mean.at[:, span(g)],
            send_sem=mean_send.at[g],
            recv_sem=mean_recv.at[g],
            device_id={"member": me + way * outward},
            device_id_type=MESH,
        )

    def partner(r):
        bit = 1 << r
        return shard + bit * (1 - 2 * ((shard // bit) % 2))

    loads = [
        pltpu.make_async_copy(prior_ref, gath.at[me], local_sem.at[0]),
        pltpu.make_async_copy(samples_ref, samples_v, local_sem.at[1]),
        pltpu.make_async_copy(noise_ref, noise_v, local_sem.at[2]),
        pltpu.make_async_copy(cells_ref, cells_v, local_sem.at[3]),
        pltpu.make_async_copy(values_ref, values_v, local_sem.at[4]),
        pltpu.make_async_copy(mask_ref, mask_v, local_sem.at[5]),
    ]
    for load in loads:
        load.start()

    barrier = pltpu.get_barrier_semaphore()

    @pl.when(me > 0)
    def _():
        pl.semaphore_signal(barrier, inc=1, device_id={"member": me - 1}, device_id_type=MESH)

    @pl.when(me < groups - 1)
    def _():
        pl.semaphore_signal(barrier, inc=1, device_id={"member": me + 1}, device_id_type=MESH)

    for r in range(rounds):
        pl.semaphore_signal(barrier, inc=1, device_id={"cell": partner(r)}, device_id_type=MESH)
    inner = (me > 0) & (me < groups - 1)

    @pl.when(inner)
    def _():
        pl.semaphore_wait(barrier, rounds + 2)

    @pl.when(jnp.logical_not(inner))
    def _():
        pl.semaphore_wait(barrier, rounds + 1)

    def goes(way, c):
        if way == 0:
            return (me < groups - 2) | ((me < groups - 1) & jnp.logical_not(left_out(c)))
        return (me > 1) | ((me > 0) & jnp.logical_not(left_out(c)))

    def send_own(c):
        for way in range(2):

            @pl.when(goes(way, c))
            def _(way=way):
                hop(way, me, c, own=True).start()

    def begin(c, _):
        send_own(c)
        return 0

    lax.fori_loop(0, AHEAD, begin, 0)

    @pl.when(end)
    def _():
        def give(g, _):
            to_helper(0, g).start()
            to_helper(1, g).start()
            return 0

        lax.fori_loop(0, GUEST, give, 0)

    for load in loads[3:]:
        load.wait()

    blocks = cells // LANES
    count_obs = cells_ref.shape[1]
    piece = min(OBS_CHUNK, count_obs)
    eye = lax.broadcasted_iota(jnp.int32, (blocks, blocks), 0) == lax.broadcasted_iota(
        jnp.int32, (blocks, blocks), 1
    )
    field_v[...] = jnp.zeros_like(field_v)
    for survey in range(cells_ref.shape[0]):

        def gather_obs(o, total, survey=survey):
            at = pl.ds(pl.multiple_of(o * piece, piece), piece)
            where = cells_v[survey : survey + 1, at] - shard * cells
            values = values_v[survey : survey + 1, at]
            block_of = where // LANES
            lane_of = where - block_of * LANES
            first = (
                lax.broadcasted_iota(jnp.int32, (blocks, piece), 0) == block_of
            )
            second = lax.broadcasted_iota(jnp.int32, (LANES, piece), 0) == lane_of
            one = values.astype(jnp.bfloat16).astype(jnp.float32)
            two = (values - one).astype(jnp.bfloat16).astype(jnp.float32)
            three = values - one - two
            left = jnp.where(first, 1.0, 0.0).astype(jnp.bfloat16)
            right = jnp.concatenate(
                [
                    jnp.where(second, part, 0.0).astype(jnp.bfloat16)
                    for part in (jnp.ones_like(values), one, two, three)
                ],
                axis=0,
            )
            return total + lax.dot_general(left, right, NT, preferred_element_type=jnp.float32)

        total = lax.fori_loop(
            0, count_obs // piece, gather_obs, jnp.zeros((blocks, 4 * LANES), jnp.float32)
        )
        flags = mask_v[survey : survey + 1, :].astype(jnp.float32)
        column = jnp.sum(jnp.where(eye, flags, 0.0), axis=1, keepdims=True)
        field_v[0] += column * total[:, :LANES]
        field_v[1] += column * (
            total[:, LANES : 2 * LANES]
            + total[:, 2 * LANES : 3 * LANES]
            + total[:, 3 * LANES : 4 * LANES]
        )

    loads[1].wait()
    loads[2].wait()
    _, _, keep0, obs0, pull0, spread0 = constants(0)
    _, _, keep1, obs1, pull1, spread1 = constants(1)

    def advance(state, fresh, precision, target):
        return (keep0 - obs0 * precision) * state + obs0 * target + spread0 * fresh

    def prepare(h, _):
        at = pl.ds(pl.multiple_of(h * LANES, LANES), LANES)
        precision = field_v[0, pl.ds(h, 1), :]
        target = field_v[1, pl.ds(h, 1), :]
        state = samples_v[:, at]
        moved = advance(state, noise_v[0, :, at], precision, target)
        factor = keep1 - obs1 * precision
        base_v[:, at] = factor * moved + obs1 * target + spread1 * noise_v[1, :, at]
        scale_v[:, at] = jnp.broadcast_to(pull0 * factor, (rows, LANES))
        high, low = split(jnp.concatenate([state, moved], axis=0))
        split_sy[: 2 * rows, at] = high
        split_sy[2 * rows :, at] = low
        return 0

    def prepare_guest(c):
        g = c // THIRD
        to_helper(0, g).wait_recv()
        to_helper(1, g).wait_recv()

        def one(k, _):
            h = c * (width // LANES) + k
            at = pl.ds(pl.multiple_of(g * width + k * LANES, LANES), LANES)
            precision = field_v[0, pl.ds(h, 1), :]
            target = field_v[1, pl.ds(h, 1), :]
            state = guest_in[0, :, at]
            moved = advance(state, guest_in[1, :, at], precision, target)
            high, low = split(jnp.concatenate([state, moved], axis=0))
            guest_sy[: 2 * rows, at] = high
            guest_sy[2 * rows :, at] = low
            return 0

        lax.fori_loop(0, width // LANES, one, 0)

    lax.fori_loop(0, blocks, prepare, 0)
    loads[0].wait()
    acc[...] = jnp.zeros_like(acc)
    guest_acc[...] = jnp.zeros_like(guest_acc)

    four = 4 * rows

    def products(c, guest):
        at = span(c)
        high, low = split(gath[:, :, at].reshape(ens, width))
        split_p[:ens, at] = high
        split_p[ens:, at] = low
        right = jnp.concatenate([high, low], axis=0)
        first = [split_sy[:, at], guest_sy[:, span(c // THIRD)]] if guest else [split_sy[:, at]]
        left = jnp.concatenate(first + [right], axis=0)
        total = guest_acc if guest else acc
        total[...] += lax.dot_general(left, right, NT, preferred_element_type=jnp.float32)

    def fold(sy, gram):
        part = jnp.concatenate(
            [sy[: 2 * rows] + sy[2 * rows :], gram[:ens] + gram[ens:]], axis=0
        )
        part = part[:, :ens] + part[:, ens:]
        half = part.shape[0] // 2
        return jnp.concatenate([part[:half], part[half:]], axis=1)

    def relay(c, d):
        missing = left_out(c)

        @pl.when((me - d >= 0) & ((me < groups - 1) | jnp.logical_not(missing)))
        def _():
            hop(1, me - d, c).wait_recv()

            @pl.when(goes(0, c))
            def _():
                hop(0, me - d, c).start()

        @pl.when((me + d < groups) & ((me > 0) | jnp.logical_not(missing)))
        def _():
            hop(0, me + d, c).wait_recv()

            @pl.when(goes(1, c))
            def _():
                hop(1, me + d, c).start()

    def step(t, _):
        @pl.when(t + AHEAD < CHUNKS)
        def _():
            send_own(t + AHEAD)

        for d in range(1, groups):
            c = t - LAG * d

            @pl.when((c >= 0) & (c < CHUNKS))
            def _(c=c, d=d):
                relay(c, d)

        c = t - LAG * furthest

        @pl.when((c >= 0) & (c < CHUNKS))
        def _():
            missing = left_out(c)

            @pl.when(missing & helper)
            def _():
                prepare_guest(c)
                products(c, True)

                @pl.when(c == THIRD * GUEST - 2)
                def _():
                    guest_part[0] = fold(guest_acc[four : 2 * four], guest_acc[2 * four :])
                    part_to_end().start()

            @pl.when(jnp.logical_not(missing & (end | helper)))
            def _():
                products(c, False)

        return 0

    lax.fori_loop(0, steps, step, 0)

    @pl.when(helper)
    def _():
        acc[:four] += guest_acc[:four]
        acc[four:] += guest_acc[2 * four :]

    outbox[0] = fold(acc[:four], acc[four:])

    @pl.when(end)
    def _():
        part_to_end(-1).wait_recv()
        outbox[0] += guest_part[1]

    part = outbox[0]
    for r in range(rounds):
        if r > 0:
            outbox[r] = part
        swap = pltpu.make_async_remote_copy(
            src_ref=outbox.at[r],
            dst_ref=inbox.at[r],
            send_sem=red_send.at[r],
            recv_sem=red_recv.at[r],
            device_id={"cell": partner(r)},
            device_id_type=MESH,
        )
        swap.start()
        swap.wait()
        part = part + inbox[r]
    part = jnp.concatenate([part[:, :ens], part[:, ens:]], axis=0)
    cross0 = part[:rows]
    cross1 = part[rows : 2 * rows]
    gram = part[2 * rows :]
    diagonal = lax.broadcasted_iota(jnp.int32, (ens, ens), 0) == lax.broadcasted_iota(
        jnp.int32, (ens, ens), 1
    )
    prior_sq = jnp.sum(jnp.where(diagonal, gram, 0.0), axis=0, keepdims=True)

    def weigh(step, cross):
        time_now, alpha = constants(step)[:2]
        dist = alpha * alpha * prior_sq - 2.0 * alpha * cross
        return softmax_rows(-dist / (2.0 * time_now * math.sqrt(ncell)))

    weights0 = weigh(0, cross0)
    cross1 = cross1 + pull0 * jnp.dot(
        weights0, gram, precision=lax.Precision.HIGHEST, preferred_element_type=jnp.float32
    )
    weights1 = weigh(1, cross1)
    weights = jnp.concatenate([weights0, weights1], axis=0)

    @pl.when(end)
    def _():
        guest_weights[0] = jnp.concatenate([weights, weights], axis=1)
        weights_to_helper().start()

    def stack(high, low):
        both = jnp.concatenate([high, low], axis=0)
        return both if both.shape[1] == 2 * ens else jnp.concatenate([both, both], axis=1)

    def means(both, c):
        at = span(c)
        mean = jnp.dot(both, split_p[:, at], preferred_element_type=jnp.float32)
        mean = mean[: 2 * rows] + mean[2 * rows :]
        return scale_v[:, at] * mean[:rows] + pull1 * mean[rows:]

    @pl.when(helper)
    def _():
        weights_to_helper().wait_recv()
        guest_both = stack(*split(guest_weights[1]))

        def serve(g, _):
            guest_out[:, span(g)] = means(guest_both, THIRD * g + 1)
            mean_to_end(g).start()
            return 0

        lax.fori_loop(0, GUEST, serve, 0)

    both = stack(*split(weights))

    def store(c):
        return pltpu.make_async_copy(
            result_v.at[:, span(c)], out_ref.at[:, span(c)], out_sem.at[c]
        )

    def finish(c, _):
        at = span(c)

        @pl.when(jnp.logical_not(end & left_out(c)))
        def _():
            result_v[:, at] = base_v[:, at] + means(both, c)
            store(c).start()

        return 0

    lax.fori_loop(0, CHUNKS, finish, 0)

    @pl.when(end)
    def _():
        def receive(g, _):
            c = THIRD * g + 1
            mean_to_end(g, -1).wait_recv()
            result_v[:, span(c)] = base_v[:, span(c)] + guest_mean[:, span(g)]
            store(c).start()
            to_helper(0, g).wait_send()
            to_helper(1, g).wait_send()
            return 0

        lax.fori_loop(0, GUEST, receive, 0)
        weights_to_helper().wait_send()

    @pl.when(helper)
    def _():
        def sent(g, _):
            mean_to_end(g).wait_send()
            return 0

        lax.fori_loop(0, GUEST, sent, 0)
        part_to_end().wait_send()

    def drain(c, _):
        store(c).wait()
        for origin in range(groups):

            @pl.when((origin <= me) & goes(0, c))
            def _(origin=origin):
                hop(0, origin, c).wait_send()

            @pl.when((origin >= me) & goes(1, c))
            def _(origin=origin):
                hop(1, origin, c).wait_send()

        return 0

    lax.fori_loop(0, CHUNKS, drain, 0)


def per_device(prior, samples, noise, obs_cells, obs_values, seismic_mask):
    rows, cells = prior.shape
    groups = lax.axis_size("member")
    shards = lax.axis_size("cell")
    ens = rows * groups
    rounds = shards.bit_length() - 1
    half = (2 * rows + ens) // 2
    held = GUEST * (cells // CHUNKS)
    hbm = pl.BlockSpec(memory_space=pltpu.HBM)
    f32 = jnp.float32
    operands = [
        pltpu.with_memory_space_constraint(x, pltpu.HBM)
        for x in (prior, samples, noise, obs_cells, obs_values, seismic_mask)
    ]
    return pl.pallas_call(
        functools.partial(kernel, groups, shards),
        out_shape=jax.ShapeDtypeStruct((rows, cells), f32),
        in_specs=[hbm] * 6,
        out_specs=pl.BlockSpec(memory_space=pl.ANY),
        scratch_shapes=[
            pltpu.VMEM(obs_cells.shape, jnp.int32),
            pltpu.VMEM(obs_values.shape, f32),
            pltpu.VMEM(seismic_mask.shape, jnp.int32),
            pltpu.VMEM((groups, rows, cells), f32),
            pltpu.VMEM((rows, cells), f32),
            pltpu.VMEM((STEPS, rows, cells), f32),
            pltpu.VMEM((4 * rows, cells), jnp.bfloat16),
            pltpu.VMEM((2 * ens, cells), jnp.bfloat16),
            pltpu.VMEM((rows, cells), f32),
            pltpu.VMEM((rows, cells), f32),
            pltpu.VMEM((rows, cells), f32),
            pltpu.VMEM((2, cells // LANES, LANES), f32),
            pltpu.VMEM((4 * rows + 2 * ens, 2 * ens), f32),
            pltpu.VMEM((rounds, half, 2 * ens), f32),
            pltpu.VMEM((rounds, half, 2 * ens), f32),
            pltpu.SemaphoreType.DMA((6,)),
            pltpu.SemaphoreType.DMA((CHUNKS,)),
            pltpu.SemaphoreType.DMA((2, groups, CHUNKS)),
            pltpu.SemaphoreType.DMA((groups, CHUNKS)),
            pltpu.SemaphoreType.DMA((rounds,)),
            pltpu.SemaphoreType.DMA((rounds,)),
            pltpu.VMEM((2, rows, held), f32),
            pltpu.VMEM((4 * rows, held), jnp.bfloat16),
            pltpu.VMEM((rows, held), f32),
            pltpu.VMEM((rows, held), f32),
            pltpu.VMEM((8 * rows + 2 * ens, 2 * ens), f32),
            pltpu.VMEM((2, half, 2 * ens), f32),
            pltpu.VMEM((2, 2 * rows, 2 * ens), f32),
            pltpu.SemaphoreType.DMA((2, GUEST)),
            pltpu.SemaphoreType.DMA((2, GUEST)),
            pltpu.SemaphoreType.DMA((2,)),
            pltpu.SemaphoreType.DMA((2,)),
            pltpu.SemaphoreType.DMA((GUEST,)),
            pltpu.SemaphoreType.DMA((GUEST,)),
        ],
        compiler_params=pltpu.CompilerParams(
            collective_id=0, has_side_effects=True, vmem_limit_bytes=48 * 1024 * 1024
        ),
    )(*operands)


def solution(mesh):
    in_specs = (
        P("member", "cell"),
        P("member", "cell"),
        P(None, "member", "cell"),
        P(None, "cell"),
        P(None, "cell"),
        P(None, "cell"),
    )
    out_specs = P("member", "cell")
    return jax.shard_map(
        per_device, mesh=mesh, in_specs=in_specs, out_specs=out_specs, check_vma=False
    )
```

```python
import functools
import math

import jax
import jax.numpy as jnp
from jax import lax
from jax.experimental import pallas as pl
from jax.experimental.pallas import tpu as pltpu
from jax.sharding import PartitionSpec as P

STEPS = 2
LANES = 128
CHUNKS = 16
THIRD = 3
GUEST = CHUNKS // THIRD
LAG = 2
AHEAD = 10
OBS_CHUNK = 512
MESH = pl.DeviceIdType.MESH
NT = (((1,), (1,)), ((), ()))


def constants(step):
    time_now = 0.6 - 0.1 * step
    alpha = 1.0 - 0.95 * time_now
    drift = -0.95 / alpha
    diffusion = 1.0 - 2.0 * drift * time_now
    keep = 1.0 - 0.1 * drift - 0.1 * diffusion / time_now
    obs = 0.1 * diffusion * (1.0 - time_now)
    pull = 0.1 * diffusion * alpha / time_now
    spread = math.sqrt(0.1 * diffusion)
    return time_now, alpha, keep, obs, pull, spread


def split(x):
    high = x.astype(jnp.bfloat16)
    low = (x - high.astype(jnp.float32)).astype(jnp.bfloat16)
    return high, low


def softmax_rows(logits):
    top = jnp.max(logits, axis=1, keepdims=True)
    e = jnp.exp(logits - top)
    return e / jnp.sum(e, axis=1, keepdims=True)


def kernel(
    groups,
    shards,
    prior_ref,
    samples_ref,
    noise_ref,
    cells_ref,
    values_ref,
    mask_ref,
    out_ref,
    cells_v,
    values_v,
    mask_v,
    gath,
    samples_v,
    noise_v,
    split_sy,
    split_p,
    base_v,
    scale_v,
    result_v,
    field_v,
    acc,
    inbox,
    outbox,
    local_sem,
    out_sem,
    send_sem,
    recv_sem,
    red_send,
    red_recv,
    guest_in,
    guest_sy,
    guest_out,
    guest_mean,
    guest_acc,
    guest_part,
    guest_weights,
    in_send,
    in_recv,
    guest_send,
    guest_recv,
    mean_send,
    mean_recv,
):
    me = lax.axis_index("member")
    shard = lax.axis_index("cell")
    rows, cells = prior_ref.shape
    ens = rows * groups
    width = cells // CHUNKS
    ncell = cells * shards
    peers = shards - 1
    low = 1 - (2 * me) // groups
    end = (me == 0) | (me == groups - 1)
    helper = (me == 1) | (me == groups - 2)
    outward = 1 - 2 * low
    furthest = me + low * (groups - 1 - 2 * me)
    steps = CHUNKS + LAG * (groups - 1)

    def span(c):
        return pl.ds(pl.multiple_of(c * width, width), width)

    def hop(way, origin, c, own=False):
        target = me + 1 if way == 0 else me - 1
        block = gath.at[origin, :, span(c)]
        return pltpu.make_async_remote_copy(
            src_ref=prior_ref.at[:, span(c)] if own else block,
            dst_ref=block,
            send_sem=send_sem.at[way, origin, c],
            recv_sem=recv_sem.at[origin, c],
            device_id={"member": target},
            device_id_type=MESH,
        )

    def left_out(c):
        return c % THIRD == 1

    def to_helper(i, g):
        source = samples_ref if i == 0 else noise_ref.at[0]
        return pltpu.make_async_remote_copy(
            src_ref=source.at[:, span(THIRD * g + 1)],
            dst_ref=guest_in.at[i, :, span(g)],
            send_sem=in_send.at[i, g],
            recv_sem=in_recv.at[i, g],
            device_id={"member": me - outward},
            device_id_type=MESH,
        )

    def part_to_end(way=1):
        return pltpu.make_async_remote_copy(
            src_ref=guest_part.at[0],
            dst_ref=guest_part.at[1],
            send_sem=guest_send.at[0],
            recv_sem=guest_recv.at[0],
            device_id={"member": me + way * outward},
            device_id_type=MESH,
        )

    def weights_to_helper():
        return pltpu.make_async_remote_copy(
            src_ref=guest_weights.at[0],
            dst_ref=guest_weights.at[1],
            send_sem=guest_send.at[1],
            recv_sem=guest_recv.at[1],
            device_id={"member": me - outward},
            device_id_type=MESH,
        )

    def mean_to_end(g, way=1):
        return pltpu.make_async_remote_copy(
            src_ref=guest_out.at[:, span(g)],
            dst_ref=guest_mean.at[:, span(g)],
            send_sem=mean_send.at[g],
            recv_sem=mean_recv.at[g],
            device_id={"member": me + way * outward},
            device_id_type=MESH,
        )

    def to_peer(k):
        return pltpu.make_async_remote_copy(
            src_ref=outbox,
            dst_ref=inbox.at[k],
            send_sem=red_send.at[k],
            recv_sem=red_recv.at[k],
            device_id={"cell": (shard + k + 1) % shards},
            device_id_type=MESH,
        )

    loads = [
        pltpu.make_async_copy(prior_ref, gath.at[me], local_sem.at[0]),
        pltpu.make_async_copy(samples_ref, samples_v, local_sem.at[1]),
        pltpu.make_async_copy(noise_ref, noise_v, local_sem.at[2]),
        pltpu.make_async_copy(cells_ref, cells_v, local_sem.at[3]),
        pltpu.make_async_copy(values_ref, values_v, local_sem.at[4]),
        pltpu.make_async_copy(mask_ref, mask_v, local_sem.at[5]),
    ]
    for load in loads:
        load.start()

    barrier = pltpu.get_barrier_semaphore()

    @pl.when(me > 0)
    def _():
        pl.semaphore_signal(barrier, inc=1, device_id={"member": me - 1}, device_id_type=MESH)

    @pl.when(me < groups - 1)
    def _():
        pl.semaphore_signal(barrier, inc=1, device_id={"member": me + 1}, device_id_type=MESH)

    for k in range(peers):
        pl.semaphore_signal(
            barrier, inc=1, device_id={"cell": (shard + k + 1) % shards}, device_id_type=MESH
        )
    inner = (me > 0) & (me < groups - 1)

    @pl.when(inner)
    def _():
        pl.semaphore_wait(barrier, peers + 2)

    @pl.when(jnp.logical_not(inner))
    def _():
        pl.semaphore_wait(barrier, peers + 1)

    def goes(way, c):
        if way == 0:
            return (me < groups - 2) | ((me < groups - 1) & jnp.logical_not(left_out(c)))
        return (me > 1) | ((me > 0) & jnp.logical_not(left_out(c)))

    def send_own(c):
        for way in range(2):

            @pl.when(goes(way, c))
            def _(way=way):
                hop(way, me, c, own=True).start()

    def begin(c, _):
        send_own(c)
        return 0

    lax.fori_loop(0, AHEAD, begin, 0)

    @pl.when(end)
    def _():
        def give(g, _):
            to_helper(0, g).start()
            to_helper(1, g).start()
            return 0

        lax.fori_loop(0, GUEST, give, 0)

    for load in loads[3:]:
        load.wait()

    blocks = cells // LANES
    count_obs = cells_ref.shape[1]
    piece = min(OBS_CHUNK, count_obs)
    eye = lax.broadcasted_iota(jnp.int32, (blocks, blocks), 0) == lax.broadcasted_iota(
        jnp.int32, (blocks, blocks), 1
    )
    field_v[...] = jnp.zeros_like(field_v)
    for survey in range(cells_ref.shape[0]):

        def gather_obs(o, total, survey=survey):
            at = pl.ds(pl.multiple_of(o * piece, piece), piece)
            where = cells_v[survey : survey + 1, at] - shard * cells
            values = values_v[survey : survey + 1, at]
            block_of = where // LANES
            lane_of = where - block_of * LANES
            first = (
                lax.broadcasted_iota(jnp.int32, (blocks, piece), 0) == block_of
            )
            second = lax.broadcasted_iota(jnp.int32, (LANES, piece), 0) == lane_of
            one = values.astype(jnp.bfloat16).astype(jnp.float32)
            two = (values - one).astype(jnp.bfloat16).astype(jnp.float32)
            three = values - one - two
            left = jnp.where(first, 1.0, 0.0).astype(jnp.bfloat16)
            right = jnp.concatenate(
                [
                    jnp.where(second, part, 0.0).astype(jnp.bfloat16)
                    for part in (jnp.ones_like(values), one, two, three)
                ],
                axis=0,
            )
            return total + lax.dot_general(left, right, NT, preferred_element_type=jnp.float32)

        total = lax.fori_loop(
            0, count_obs // piece, gather_obs, jnp.zeros((blocks, 4 * LANES), jnp.float32)
        )
        flags = mask_v[survey : survey + 1, :].astype(jnp.float32)
        column = jnp.sum(jnp.where(eye, flags, 0.0), axis=1, keepdims=True)
        field_v[0] += column * total[:, :LANES]
        field_v[1] += column * (
            total[:, LANES : 2 * LANES]
            + total[:, 2 * LANES : 3 * LANES]
            + total[:, 3 * LANES : 4 * LANES]
        )

    loads[1].wait()
    loads[2].wait()
    _, _, keep0, obs0, pull0, spread0 = constants(0)
    _, _, keep1, obs1, pull1, spread1 = constants(1)

    def advance(state, fresh, precision, target):
        return (keep0 - obs0 * precision) * state + obs0 * target + spread0 * fresh

    def prepare(h, _):
        at = pl.ds(pl.multiple_of(h * LANES, LANES), LANES)
        precision = field_v[0, pl.ds(h, 1), :]
        target = field_v[1, pl.ds(h, 1), :]
        state = samples_v[:, at]
        moved = advance(state, noise_v[0, :, at], precision, target)
        factor = keep1 - obs1 * precision
        base_v[:, at] = factor * moved + obs1 * target + spread1 * noise_v[1, :, at]
        scale_v[:, at] = jnp.broadcast_to(pull0 * factor, (rows, LANES))
        high, low = split(jnp.concatenate([state, moved], axis=0))
        split_sy[: 2 * rows, at] = high
        split_sy[2 * rows :, at] = low
        return 0

    def prepare_guest(c):
        g = c // THIRD
        to_helper(0, g).wait_recv()
        to_helper(1, g).wait_recv()

        def one(k, _):
            h = c * (width // LANES) + k
            at = pl.ds(pl.multiple_of(g * width + k * LANES, LANES), LANES)
            precision = field_v[0, pl.ds(h, 1), :]
            target = field_v[1, pl.ds(h, 1), :]
            state = guest_in[0, :, at]
            moved = advance(state, guest_in[1, :, at], precision, target)
            high, low = split(jnp.concatenate([state, moved], axis=0))
            guest_sy[: 2 * rows, at] = high
            guest_sy[2 * rows :, at] = low
            return 0

        lax.fori_loop(0, width // LANES, one, 0)

    loads[0].wait()
    acc[...] = jnp.zeros_like(acc)
    guest_acc[...] = jnp.zeros_like(guest_acc)

    four = 4 * rows

    def products(c, guest):
        at = span(c)
        high, low = split(gath[:, :, at].reshape(ens, width))
        split_p[:ens, at] = high
        split_p[ens:, at] = low
        right = jnp.concatenate([high, low], axis=0)
        first = [split_sy[:, at], guest_sy[:, span(c // THIRD)]] if guest else [split_sy[:, at]]
        left = jnp.concatenate(first + [right], axis=0)
        total = guest_acc if guest else acc
        total[...] += lax.dot_general(left, right, NT, preferred_element_type=jnp.float32)

    def fold(sy, gram):
        part = jnp.concatenate(
            [sy[: 2 * rows] + sy[2 * rows :], gram[:ens] + gram[ens:]], axis=0
        )
        part = part[:, :ens] + part[:, ens:]
        half = part.shape[0] // 2
        return jnp.concatenate([part[:half], part[half:]], axis=1)

    def relay(c, d):
        missing = left_out(c)

        @pl.when((me - d >= 0) & ((me < groups - 1) | jnp.logical_not(missing)))
        def _():
            hop(1, me - d, c).wait_recv()

            @pl.when(goes(0, c))
            def _():
                hop(0, me - d, c).start()

        @pl.when((me + d < groups) & ((me > 0) | jnp.logical_not(missing)))
        def _():
            hop(0, me + d, c).wait_recv()

            @pl.when(goes(1, c))
            def _():
                hop(1, me + d, c).start()

    def step(t, _):
        @pl.when(t + AHEAD < CHUNKS)
        def _():
            send_own(t + AHEAD)

        for d in range(1, groups):
            c = t - LAG * d

            @pl.when((c >= 0) & (c < CHUNKS))
            def _(c=c, d=d):
                relay(c, d)

        @pl.when(t < CHUNKS)
        def _():
            per = width // LANES
            lax.fori_loop(t * per, t * per + per, prepare, 0)

        c = t - LAG * furthest

        @pl.when((c >= 0) & (c < CHUNKS))
        def _():
            missing = left_out(c)

            @pl.when(missing & helper)
            def _():
                prepare_guest(c)
                products(c, True)

                @pl.when(c == THIRD * GUEST - 2)
                def _():
                    guest_part[0] = fold(guest_acc[four : 2 * four], guest_acc[2 * four :])
                    part_to_end().start()

            @pl.when(jnp.logical_not(missing & (end | helper)))
            def _():
                products(c, False)

        return 0

    lax.fori_loop(0, steps, step, 0)

    @pl.when(helper)
    def _():
        acc[:four] += guest_acc[:four]
        acc[four:] += guest_acc[2 * four :]

    outbox[...] = fold(acc[:four], acc[four:])

    @pl.when(end)
    def _():
        part_to_end(-1).wait_recv()
        outbox[...] += guest_part[1]

    for k in range(peers):
        to_peer(k).start()
    part = outbox[...]
    for k in range(peers):
        to_peer(k).wait_recv()
        part = part + inbox[k]
    part = jnp.concatenate([part[:, :ens], part[:, ens:]], axis=0)
    cross0 = part[:rows]
    cross1 = part[rows : 2 * rows]
    gram = part[2 * rows :]
    diagonal = lax.broadcasted_iota(jnp.int32, (ens, ens), 0) == lax.broadcasted_iota(
        jnp.int32, (ens, ens), 1
    )
    prior_sq = jnp.sum(jnp.where(diagonal, gram, 0.0), axis=0, keepdims=True)

    def weigh(step, cross):
        time_now, alpha = constants(step)[:2]
        dist = alpha * alpha * prior_sq - 2.0 * alpha * cross
        return softmax_rows(-dist / (2.0 * time_now * math.sqrt(ncell)))

    weights0 = weigh(0, cross0)
    cross1 = cross1 + pull0 * jnp.dot(
        weights0, gram, precision=lax.Precision.HIGHEST, preferred_element_type=jnp.float32
    )
    weights1 = weigh(1, cross1)
    weights = jnp.concatenate([weights0, weights1], axis=0)

    @pl.when(end)
    def _():
        guest_weights[0] = jnp.concatenate([weights, weights], axis=1)
        weights_to_helper().start()

    def stack(high, low):
        both = jnp.concatenate([high, low], axis=0)
        return both if both.shape[1] == 2 * ens else jnp.concatenate([both, both], axis=1)

    def means(both, c):
        at = span(c)
        mean = jnp.dot(both, split_p[:, at], preferred_element_type=jnp.float32)
        mean = mean[: 2 * rows] + mean[2 * rows :]
        return scale_v[:, at] * mean[:rows] + pull1 * mean[rows:]

    @pl.when(helper)
    def _():
        weights_to_helper().wait_recv()
        guest_both = stack(*split(guest_weights[1]))

        def serve(g, _):
            guest_out[:, span(g)] = means(guest_both, THIRD * g + 1)
            mean_to_end(g).start()
            return 0

        lax.fori_loop(0, GUEST, serve, 0)

    both = stack(*split(weights))

    def store(c):
        return pltpu.make_async_copy(
            result_v.at[:, span(c)], out_ref.at[:, span(c)], out_sem.at[c]
        )

    def finish(c, _):
        at = span(c)

        @pl.when(jnp.logical_not(end & left_out(c)))
        def _():
            result_v[:, at] = base_v[:, at] + means(both, c)
            store(c).start()

        return 0

    lax.fori_loop(0, CHUNKS, finish, 0)

    @pl.when(end)
    def _():
        def receive(g, _):
            c = THIRD * g + 1
            mean_to_end(g, -1).wait_recv()
            result_v[:, span(c)] = base_v[:, span(c)] + guest_mean[:, span(g)]
            store(c).start()
            to_helper(0, g).wait_send()
            to_helper(1, g).wait_send()
            return 0

        lax.fori_loop(0, GUEST, receive, 0)
        weights_to_helper().wait_send()

    @pl.when(helper)
    def _():
        def sent(g, _):
            mean_to_end(g).wait_send()
            return 0

        lax.fori_loop(0, GUEST, sent, 0)
        part_to_end().wait_send()

    def drain(c, _):
        store(c).wait()
        for origin in range(groups):

            @pl.when((origin <= me) & goes(0, c))
            def _(origin=origin):
                hop(0, origin, c).wait_send()

            @pl.when((origin >= me) & goes(1, c))
            def _(origin=origin):
                hop(1, origin, c).wait_send()

        return 0

    lax.fori_loop(0, CHUNKS, drain, 0)
    for k in range(peers):
        to_peer(k).wait_send()


def per_device(prior, samples, noise, obs_cells, obs_values, seismic_mask):
    rows, cells = prior.shape
    groups = lax.axis_size("member")
    shards = lax.axis_size("cell")
    ens = rows * groups
    peers = shards - 1
    half = (2 * rows + ens) // 2
    held = GUEST * (cells // CHUNKS)
    hbm = pl.BlockSpec(memory_space=pltpu.HBM)
    f32 = jnp.float32
    operands = [
        pltpu.with_memory_space_constraint(x, pltpu.HBM)
        for x in (prior, samples, noise, obs_cells, obs_values, seismic_mask)
    ]
    return pl.pallas_call(
        functools.partial(kernel, groups, shards),
        out_shape=jax.ShapeDtypeStruct((rows, cells), f32),
        in_specs=[hbm] * 6,
        out_specs=pl.BlockSpec(memory_space=pl.ANY),
        scratch_shapes=[
            pltpu.VMEM(obs_cells.shape, jnp.int32),
            pltpu.VMEM(obs_values.shape, f32),
            pltpu.VMEM(seismic_mask.shape, jnp.int32),
            pltpu.VMEM((groups, rows, cells), f32),
            pltpu.VMEM((rows, cells), f32),
            pltpu.VMEM((STEPS, rows, cells), f32),
            pltpu.VMEM((4 * rows, cells), jnp.bfloat16),
            pltpu.VMEM((2 * ens, cells), jnp.bfloat16),
            pltpu.VMEM((rows, cells), f32),
            pltpu.VMEM((rows, cells), f32),
            pltpu.VMEM((rows, cells), f32),
            pltpu.VMEM((2, cells // LANES, LANES), f32),
            pltpu.VMEM((4 * rows + 2 * ens, 2 * ens), f32),
            pltpu.VMEM((peers, half, 2 * ens), f32),
            pltpu.VMEM((half, 2 * ens), f32),
            pltpu.SemaphoreType.DMA((6,)),
            pltpu.SemaphoreType.DMA((CHUNKS,)),
            pltpu.SemaphoreType.DMA((2, groups, CHUNKS)),
            pltpu.SemaphoreType.DMA((groups, CHUNKS)),
            pltpu.SemaphoreType.DMA((peers,)),
            pltpu.SemaphoreType.DMA((peers,)),
            pltpu.VMEM((2, rows, held), f32),
            pltpu.VMEM((4 * rows, held), jnp.bfloat16),
            pltpu.VMEM((rows, held), f32),
            pltpu.VMEM((rows, held), f32),
            pltpu.VMEM((8 * rows + 2 * ens, 2 * ens), f32),
            pltpu.VMEM((2, half, 2 * ens), f32),
            pltpu.VMEM((2, 2 * rows, 2 * ens), f32),
            pltpu.SemaphoreType.DMA((2, GUEST)),
            pltpu.SemaphoreType.DMA((2, GUEST)),
            pltpu.SemaphoreType.DMA((2,)),
            pltpu.SemaphoreType.DMA((2,)),
            pltpu.SemaphoreType.DMA((GUEST,)),
            pltpu.SemaphoreType.DMA((GUEST,)),
        ],
        compiler_params=pltpu.CompilerParams(
            collective_id=0, has_side_effects=True, vmem_limit_bytes=48 * 1024 * 1024
        ),
    )(*operands)


def solution(mesh):
    in_specs = (
        P("member", "cell"),
        P("member", "cell"),
        P(None, "member", "cell"),
        P(None, "cell"),
        P(None, "cell"),
        P(None, "cell"),
    )
    out_specs = P("member", "cell")
    return jax.shard_map(
        per_device, mesh=mesh, in_specs=in_specs, out_specs=out_specs, check_vma=False
    )
```

```python
import functools
import math

import jax
import jax.numpy as jnp
from jax import lax
from jax.experimental import pallas as pl
from jax.experimental.pallas import tpu as pltpu
from jax.sharding import PartitionSpec as P

STEPS = 2
LANES = 128
CHUNKS = 16
THIRD = 3
GUEST = CHUNKS // THIRD
SERVED = GUEST - 2
LAG = 2
AHEAD = 10
OBS_CHUNK = 512
MESH = pl.DeviceIdType.MESH
NT = (((1,), (1,)), ((), ()))


def constants(step):
    time_now = 0.6 - 0.1 * step
    alpha = 1.0 - 0.95 * time_now
    drift = -0.95 / alpha
    diffusion = 1.0 - 2.0 * drift * time_now
    keep = 1.0 - 0.1 * drift - 0.1 * diffusion / time_now
    obs = 0.1 * diffusion * (1.0 - time_now)
    pull = 0.1 * diffusion * alpha / time_now
    spread = math.sqrt(0.1 * diffusion)
    return time_now, alpha, keep, obs, pull, spread


def split(x):
    high = x.astype(jnp.bfloat16)
    low = (x - high.astype(jnp.float32)).astype(jnp.bfloat16)
    return high, low


def softmax_rows(logits):
    top = jnp.max(logits, axis=1, keepdims=True)
    e = jnp.exp(logits - top)
    return e / jnp.sum(e, axis=1, keepdims=True)


def kernel(
    groups,
    shards,
    prior_ref,
    samples_ref,
    noise_ref,
    cells_ref,
    values_ref,
    mask_ref,
    out_ref,
    cells_v,
    values_v,
    mask_v,
    gath,
    samples_v,
    noise_v,
    split_sy,
    split_p,
    base_v,
    scale_v,
    result_v,
    field_v,
    acc,
    inbox,
    outbox,
    local_sem,
    out_sem,
    send_sem,
    recv_sem,
    red_send,
    red_recv,
    guest_in,
    guest_sy,
    guest_out,
    guest_mean,
    guest_acc,
    guest_part,
    guest_weights,
    in_send,
    in_recv,
    guest_send,
    guest_recv,
    mean_send,
    mean_recv,
):
    me = lax.axis_index("member")
    shard = lax.axis_index("cell")
    rows, cells = prior_ref.shape
    ens = rows * groups
    width = cells // CHUNKS
    ncell = cells * shards
    peers = shards - 1
    low = 1 - (2 * me) // groups
    end = (me == 0) | (me == groups - 1)
    helper = (me == 1) | (me == groups - 2)
    outward = 1 - 2 * low
    furthest = me + low * (groups - 1 - 2 * me)
    steps = CHUNKS + LAG * (groups - 1)

    def span(c):
        return pl.ds(c * width if isinstance(c, int) else pl.multiple_of(c * width, width), width)

    def hop(way, origin, c, own=False):
        target = me + 1 if way == 0 else me - 1
        block = gath.at[origin, :, span(c)]
        return pltpu.make_async_remote_copy(
            src_ref=prior_ref.at[:, span(c)] if own else block,
            dst_ref=block,
            send_sem=send_sem.at[way, origin, c],
            recv_sem=recv_sem.at[origin, c],
            device_id={"member": target},
            device_id_type=MESH,
        )

    def left_out(c):
        return c % THIRD == 1

    def to_helper(i, g):
        source = samples_ref if i == 0 else noise_ref.at[0]
        return pltpu.make_async_remote_copy(
            src_ref=source.at[:, span(THIRD * g + 1)],
            dst_ref=guest_in.at[i, :, span(g)],
            send_sem=in_send.at[i, g],
            recv_sem=in_recv.at[i, g],
            device_id={"member": me - outward},
            device_id_type=MESH,
        )

    def part_to_end(way=1):
        return pltpu.make_async_remote_copy(
            src_ref=guest_part.at[0],
            dst_ref=guest_part.at[1],
            send_sem=guest_send.at[0],
            recv_sem=guest_recv.at[0],
            device_id={"member": me + way * outward},
            device_id_type=MESH,
        )

    def weights_to_helper():
        return pltpu.make_async_remote_copy(
            src_ref=guest_weights.at[0],
            dst_ref=guest_weights.at[1],
            send_sem=guest_send.at[1],
            recv_sem=guest_recv.at[1],
            device_id={"member": me - outward},
            device_id_type=MESH,
        )

    def mean_to_end(g, way=1):
        return pltpu.make_async_remote_copy(
            src_ref=guest_out.at[:, span(g)],
            dst_ref=guest_mean.at[:, span(g)],
            send_sem=mean_send.at[g],
            recv_sem=mean_recv.at[g],
            device_id={"member": me + way * outward},
            device_id_type=MESH,
        )

    def to_peer(k):
        return pltpu.make_async_remote_copy(
            src_ref=outbox,
            dst_ref=inbox.at[k],
            send_sem=red_send.at[k],
            recv_sem=red_recv.at[k],
            device_id={"cell": (shard + k + 1) % shards},
            device_id_type=MESH,
        )

    loads = [
        pltpu.make_async_copy(prior_ref, gath.at[me], local_sem.at[0]),
        pltpu.make_async_copy(samples_ref, samples_v, local_sem.at[1]),
        pltpu.make_async_copy(noise_ref, noise_v, local_sem.at[2]),
        pltpu.make_async_copy(cells_ref, cells_v, local_sem.at[3]),
        pltpu.make_async_copy(values_ref, values_v, local_sem.at[4]),
        pltpu.make_async_copy(mask_ref, mask_v, local_sem.at[5]),
    ]
    for load in loads:
        load.start()

    barrier = pltpu.get_barrier_semaphore()

    @pl.when(me > 0)
    def _():
        pl.semaphore_signal(barrier, inc=1, device_id={"member": me - 1}, device_id_type=MESH)

    @pl.when(me < groups - 1)
    def _():
        pl.semaphore_signal(barrier, inc=1, device_id={"member": me + 1}, device_id_type=MESH)

    for k in range(peers):
        pl.semaphore_signal(
            barrier, inc=1, device_id={"cell": (shard + k + 1) % shards}, device_id_type=MESH
        )
    inner = (me > 0) & (me < groups - 1)

    @pl.when(inner)
    def _():
        pl.semaphore_wait(barrier, peers + 2)

    @pl.when(jnp.logical_not(inner))
    def _():
        pl.semaphore_wait(barrier, peers + 1)

    def goes(way, c):
        if way == 0:
            return (me < groups - 2) | ((me < groups - 1) & jnp.logical_not(left_out(c)))
        return (me > 1) | ((me > 0) & jnp.logical_not(left_out(c)))

    def send_own(c):
        for way in range(2):

            @pl.when(goes(way, c))
            def _(way=way):
                hop(way, me, c, own=True).start()

    def begin(c, _):
        send_own(c)
        return 0

    lax.fori_loop(0, AHEAD, begin, 0)

    @pl.when(end)
    def _():
        def give(g, _):
            to_helper(0, g).start()
            to_helper(1, g).start()
            return 0

        lax.fori_loop(0, GUEST, give, 0)

    for load in loads[3:]:
        load.wait()

    blocks = cells // LANES
    count_obs = cells_ref.shape[1]
    piece = min(OBS_CHUNK, count_obs)
    eye = lax.broadcasted_iota(jnp.int32, (blocks, blocks), 0) == lax.broadcasted_iota(
        jnp.int32, (blocks, blocks), 1
    )
    field_v[...] = jnp.zeros_like(field_v)
    for survey in range(cells_ref.shape[0]):

        def gather_obs(o, total, survey=survey):
            at = pl.ds(pl.multiple_of(o * piece, piece), piece)
            where = cells_v[survey : survey + 1, at] - shard * cells
            values = values_v[survey : survey + 1, at]
            block_of = where // LANES
            lane_of = where - block_of * LANES
            first = (
                lax.broadcasted_iota(jnp.int32, (blocks, piece), 0) == block_of
            )
            second = lax.broadcasted_iota(jnp.int32, (LANES, piece), 0) == lane_of
            one = values.astype(jnp.bfloat16).astype(jnp.float32)
            two = (values - one).astype(jnp.bfloat16).astype(jnp.float32)
            three = values - one - two
            left = jnp.where(first, 1.0, 0.0).astype(jnp.bfloat16)
            right = jnp.concatenate(
                [
                    jnp.where(second, part, 0.0).astype(jnp.bfloat16)
                    for part in (jnp.ones_like(values), one, two, three)
                ],
                axis=0,
            )
            return total + lax.dot_general(left, right, NT, preferred_element_type=jnp.float32)

        total = lax.fori_loop(
            0, count_obs // piece, gather_obs, jnp.zeros((blocks, 4 * LANES), jnp.float32)
        )
        flags = mask_v[survey : survey + 1, :].astype(jnp.float32)
        column = jnp.sum(jnp.where(eye, flags, 0.0), axis=1, keepdims=True)
        field_v[0] += column * total[:, :LANES]
        field_v[1] += column * (
            total[:, LANES : 2 * LANES]
            + total[:, 2 * LANES : 3 * LANES]
            + total[:, 3 * LANES : 4 * LANES]
        )

    loads[1].wait()
    loads[2].wait()
    _, _, keep0, obs0, pull0, spread0 = constants(0)
    _, _, keep1, obs1, pull1, spread1 = constants(1)

    def advance(state, fresh, precision, target):
        return (keep0 - obs0 * precision) * state + obs0 * target + spread0 * fresh

    def prepare(h, _):
        at = pl.ds(pl.multiple_of(h * LANES, LANES), LANES)
        precision = field_v[0, pl.ds(h, 1), :]
        target = field_v[1, pl.ds(h, 1), :]
        state = samples_v[:, at]
        moved = advance(state, noise_v[0, :, at], precision, target)
        factor = keep1 - obs1 * precision
        base_v[:, at] = factor * moved + obs1 * target + spread1 * noise_v[1, :, at]
        scale_v[:, at] = jnp.broadcast_to(pull0 * factor, (rows, LANES))
        high, low = split(jnp.concatenate([state, moved], axis=0))
        split_sy[: 2 * rows, at] = high
        split_sy[2 * rows :, at] = low
        return 0

    def prepare_guest(c):
        g = c // THIRD
        to_helper(0, g).wait_recv()
        to_helper(1, g).wait_recv()

        def one(k, _):
            h = c * (width // LANES) + k
            at = pl.ds(pl.multiple_of(g * width + k * LANES, LANES), LANES)
            precision = field_v[0, pl.ds(h, 1), :]
            target = field_v[1, pl.ds(h, 1), :]
            state = guest_in[0, :, at]
            moved = advance(state, guest_in[1, :, at], precision, target)
            high, low = split(jnp.concatenate([state, moved], axis=0))
            guest_sy[: 2 * rows, at] = high
            guest_sy[2 * rows :, at] = low
            return 0

        lax.fori_loop(0, width // LANES, one, 0)

    loads[0].wait()
    acc[...] = jnp.zeros_like(acc)
    guest_acc[...] = jnp.zeros_like(guest_acc)

    four = 4 * rows

    def products(c, guest):
        at = span(c)
        high, low = split(gath[:, :, at].reshape(ens, width))
        split_p[:ens, at] = high
        split_p[ens:, at] = low
        right = jnp.concatenate([high, low], axis=0)
        first = [split_sy[:, at], guest_sy[:, span(c // THIRD)]] if guest else [split_sy[:, at]]
        left = jnp.concatenate(first + [right], axis=0)
        total = guest_acc if guest else acc
        total[...] += lax.dot_general(left, right, NT, preferred_element_type=jnp.float32)

    def fold(sy, gram):
        part = jnp.concatenate(
            [sy[: 2 * rows] + sy[2 * rows :], gram[:ens] + gram[ens:]], axis=0
        )
        part = part[:, :ens] + part[:, ens:]
        half = part.shape[0] // 2
        return jnp.concatenate([part[:half], part[half:]], axis=1)

    def relay(c, d):
        missing = left_out(c)

        @pl.when((me - d >= 0) & ((me < groups - 1) | jnp.logical_not(missing)))
        def _():
            hop(1, me - d, c).wait_recv()

            @pl.when(goes(0, c))
            def _():
                hop(0, me - d, c).start()

        @pl.when((me + d < groups) & ((me > 0) | jnp.logical_not(missing)))
        def _():
            hop(0, me + d, c).wait_recv()

            @pl.when(goes(1, c))
            def _():
                hop(1, me + d, c).start()

    def step(t, _):
        @pl.when(t + AHEAD < CHUNKS)
        def _():
            send_own(t + AHEAD)

        for d in range(1, groups):
            c = t - LAG * d

            @pl.when((c >= 0) & (c < CHUNKS))
            def _(c=c, d=d):
                relay(c, d)

        @pl.when(t < CHUNKS)
        def _():
            per = width // LANES
            lax.fori_loop(t * per, t * per + per, prepare, 0)

        c = t - LAG * furthest

        @pl.when((c >= 0) & (c < CHUNKS))
        def _():
            missing = left_out(c)

            @pl.when(missing & helper)
            def _():
                prepare_guest(c)
                products(c, True)

                @pl.when(c == THIRD * GUEST - 2)
                def _():
                    guest_part[0] = fold(guest_acc[four : 2 * four], guest_acc[2 * four :])
                    part_to_end().start()

            @pl.when(jnp.logical_not(missing & (end | helper)))
            def _():
                products(c, False)

        return 0

    lax.fori_loop(0, steps, step, 0)

    late = [THIRD * g + 1 for g in range(SERVED, GUEST)]

    @pl.when(me == 1)
    def _():
        for c in late:
            for origin in range(1, groups):
                hop(1, origin, c).start()

    @pl.when(me == groups - 2)
    def _():
        for c in late:
            for origin in range(groups - 1):
                hop(0, origin, c).start()

    @pl.when(helper)
    def _():
        acc[:four] += guest_acc[:four]
        acc[four:] += guest_acc[2 * four :]

    outbox[...] = fold(acc[:four], acc[four:])

    @pl.when(end)
    def _():
        part_to_end(-1).wait_recv()
        outbox[...] += guest_part[1]

    for k in range(peers):
        to_peer(k).start()
    part = outbox[...]
    for k in range(peers):
        to_peer(k).wait_recv()
        part = part + inbox[k]
    part = jnp.concatenate([part[:, :ens], part[:, ens:]], axis=0)
    cross0 = part[:rows]
    cross1 = part[rows : 2 * rows]
    gram = part[2 * rows :]
    diagonal = lax.broadcasted_iota(jnp.int32, (ens, ens), 0) == lax.broadcasted_iota(
        jnp.int32, (ens, ens), 1
    )
    prior_sq = jnp.sum(jnp.where(diagonal, gram, 0.0), axis=0, keepdims=True)

    def weigh(step, cross):
        time_now, alpha = constants(step)[:2]
        dist = alpha * alpha * prior_sq - 2.0 * alpha * cross
        return softmax_rows(-dist / (2.0 * time_now * math.sqrt(ncell)))

    weights0 = weigh(0, cross0)
    cross1 = cross1 + pull0 * jnp.dot(
        weights0, gram, precision=lax.Precision.HIGHEST, preferred_element_type=jnp.float32
    )
    weights1 = weigh(1, cross1)
    weights = jnp.concatenate([weights0, weights1], axis=0)

    @pl.when(end)
    def _():
        guest_weights[0] = jnp.concatenate([weights, weights], axis=1)
        weights_to_helper().start()

    def stack(high, low):
        both = jnp.concatenate([high, low], axis=0)
        return both if both.shape[1] == 2 * ens else jnp.concatenate([both, both], axis=1)

    def means(both, c):
        at = span(c)
        mean = jnp.dot(both, split_p[:, at], preferred_element_type=jnp.float32)
        mean = mean[: 2 * rows] + mean[2 * rows :]
        return scale_v[:, at] * mean[:rows] + pull1 * mean[rows:]

    @pl.when(helper)
    def _():
        weights_to_helper().wait_recv()
        guest_both = stack(*split(guest_weights[1]))

        def serve(g, _):
            guest_out[:, span(g)] = means(guest_both, THIRD * g + 1)
            mean_to_end(g).start()
            return 0

        lax.fori_loop(0, SERVED, serve, 0)

    both = stack(*split(weights))

    def store(c):
        return pltpu.make_async_copy(
            result_v.at[:, span(c)], out_ref.at[:, span(c)], out_sem.at[c]
        )

    def finish(c, _):
        at = span(c)

        @pl.when(jnp.logical_not(end & left_out(c)))
        def _():
            result_v[:, at] = base_v[:, at] + means(both, c)
            store(c).start()

        return 0

    lax.fori_loop(0, CHUNKS, finish, 0)

    @pl.when(end)
    def _():
        def receive(g, _):
            c = THIRD * g + 1
            mean_to_end(g, -1).wait_recv()
            result_v[:, span(c)] = base_v[:, span(c)] + guest_mean[:, span(g)]
            store(c).start()
            return 0

        def taken(g, _):
            to_helper(0, g).wait_send()
            to_helper(1, g).wait_send()
            return 0

        for c in late:

            @pl.when(me == 0)
            def _(c=c):
                for origin in range(1, groups):
                    hop(0, origin, c).wait_recv()

            @pl.when(me == groups - 1)
            def _(c=c):
                for origin in range(groups - 1):
                    hop(1, origin, c).wait_recv()

            high, low = split(gath[:, :, span(c)].reshape(ens, width))
            split_p[:ens, span(c)] = high
            split_p[ens:, span(c)] = low
            result_v[:, span(c)] = base_v[:, span(c)] + means(both, c)
            store(c).start()
        lax.fori_loop(0, SERVED, receive, 0)
        lax.fori_loop(0, GUEST, taken, 0)
        weights_to_helper().wait_send()

    @pl.when(helper)
    def _():
        def sent(g, _):
            mean_to_end(g).wait_send()
            return 0

        lax.fori_loop(0, SERVED, sent, 0)
        part_to_end().wait_send()

    def drain(c, _):
        store(c).wait()
        for origin in range(groups):

            @pl.when((origin <= me) & goes(0, c))
            def _(origin=origin):
                hop(0, origin, c).wait_send()

            @pl.when((origin >= me) & goes(1, c))
            def _(origin=origin):
                hop(1, origin, c).wait_send()

        return 0

    lax.fori_loop(0, CHUNKS, drain, 0)

    @pl.when(me == 1)
    def _():
        for c in late:
            for origin in range(1, groups):
                hop(1, origin, c).wait_send()

    @pl.when(me == groups - 2)
    def _():
        for c in late:
            for origin in range(groups - 1):
                hop(0, origin, c).wait_send()

    for k in range(peers):
        to_peer(k).wait_send()


def per_device(prior, samples, noise, obs_cells, obs_values, seismic_mask):
    rows, cells = prior.shape
    groups = lax.axis_size("member")
    shards = lax.axis_size("cell")
    ens = rows * groups
    peers = shards - 1
    half = (2 * rows + ens) // 2
    held = GUEST * (cells // CHUNKS)
    hbm = pl.BlockSpec(memory_space=pltpu.HBM)
    f32 = jnp.float32
    operands = [
        pltpu.with_memory_space_constraint(x, pltpu.HBM)
        for x in (prior, samples, noise, obs_cells, obs_values, seismic_mask)
    ]
    return pl.pallas_call(
        functools.partial(kernel, groups, shards),
        out_shape=jax.ShapeDtypeStruct((rows, cells), f32),
        in_specs=[hbm] * 6,
        out_specs=pl.BlockSpec(memory_space=pl.ANY),
        scratch_shapes=[
            pltpu.VMEM(obs_cells.shape, jnp.int32),
            pltpu.VMEM(obs_values.shape, f32),
            pltpu.VMEM(seismic_mask.shape, jnp.int32),
            pltpu.VMEM((groups, rows, cells), f32),
            pltpu.VMEM((rows, cells), f32),
            pltpu.VMEM((STEPS, rows, cells), f32),
            pltpu.VMEM((4 * rows, cells), jnp.bfloat16),
            pltpu.VMEM((2 * ens, cells), jnp.bfloat16),
            pltpu.VMEM((rows, cells), f32),
            pltpu.VMEM((rows, cells), f32),
            pltpu.VMEM((rows, cells), f32),
            pltpu.VMEM((2, cells // LANES, LANES), f32),
            pltpu.VMEM((4 * rows + 2 * ens, 2 * ens), f32),
            pltpu.VMEM((peers, half, 2 * ens), f32),
            pltpu.VMEM((half, 2 * ens), f32),
            pltpu.SemaphoreType.DMA((6,)),
            pltpu.SemaphoreType.DMA((CHUNKS,)),
            pltpu.SemaphoreType.DMA((2, groups, CHUNKS)),
            pltpu.SemaphoreType.DMA((groups, CHUNKS)),
            pltpu.SemaphoreType.DMA((peers,)),
            pltpu.SemaphoreType.DMA((peers,)),
            pltpu.VMEM((2, rows, held), f32),
            pltpu.VMEM((4 * rows, held), jnp.bfloat16),
            pltpu.VMEM((rows, held), f32),
            pltpu.VMEM((rows, held), f32),
            pltpu.VMEM((8 * rows + 2 * ens, 2 * ens), f32),
            pltpu.VMEM((2, half, 2 * ens), f32),
            pltpu.VMEM((2, 2 * rows, 2 * ens), f32),
            pltpu.SemaphoreType.DMA((2, GUEST)),
            pltpu.SemaphoreType.DMA((2, GUEST)),
            pltpu.SemaphoreType.DMA((2,)),
            pltpu.SemaphoreType.DMA((2,)),
            pltpu.SemaphoreType.DMA((GUEST,)),
            pltpu.SemaphoreType.DMA((GUEST,)),
        ],
        compiler_params=pltpu.CompilerParams(
            collective_id=0, has_side_effects=True, vmem_limit_bytes=48 * 1024 * 1024
        ),
    )(*operands)


def solution(mesh):
    in_specs = (
        P("member", "cell"),
        P("member", "cell"),
        P(None, "member", "cell"),
        P(None, "cell"),
        P(None, "cell"),
        P(None, "cell"),
    )
    out_specs = P("member", "cell")
    return jax.shard_map(
        per_device, mesh=mesh, in_specs=in_specs, out_specs=out_specs, check_vma=False
    )
```

```python
import functools
import math

import jax
import jax.numpy as jnp
from jax import lax
from jax.experimental import pallas as pl
from jax.experimental.pallas import tpu as pltpu
from jax.sharding import PartitionSpec as P

STEPS = 2
LANES = 128
CHUNKS = 16
THIRD = 3
GUEST = CHUNKS // THIRD
SERVED = GUEST - 2
LAG = 2
AHEAD = 10
OBS_CHUNK = 512
MESH = pl.DeviceIdType.MESH
NT = (((1,), (1,)), ((), ()))


def constants(step):
    time_now = 0.6 - 0.1 * step
    alpha = 1.0 - 0.95 * time_now
    drift = -0.95 / alpha
    diffusion = 1.0 - 2.0 * drift * time_now
    keep = 1.0 - 0.1 * drift - 0.1 * diffusion / time_now
    obs = 0.1 * diffusion * (1.0 - time_now)
    pull = 0.1 * diffusion * alpha / time_now
    spread = math.sqrt(0.1 * diffusion)
    return time_now, alpha, keep, obs, pull, spread


def split(x):
    high = x.astype(jnp.bfloat16)
    low = (x - high.astype(jnp.float32)).astype(jnp.bfloat16)
    return high, low


def softmax_rows(logits):
    top = jnp.max(logits, axis=1, keepdims=True)
    e = jnp.exp(logits - top)
    return e / jnp.sum(e, axis=1, keepdims=True)


def kernel(
    groups,
    shards,
    prior_ref,
    samples_ref,
    noise_ref,
    cells_ref,
    values_ref,
    mask_ref,
    out_ref,
    cells_v,
    values_v,
    mask_v,
    gath,
    samples_v,
    noise_v,
    split_sy,
    split_p,
    base_v,
    scale_v,
    result_v,
    field_v,
    acc,
    inbox,
    outbox,
    local_sem,
    out_sem,
    send_sem,
    recv_sem,
    red_send,
    red_recv,
    guest_in,
    guest_sy,
    guest_out,
    guest_mean,
    guest_acc,
    guest_part,
    guest_weights,
    in_send,
    in_recv,
    guest_send,
    guest_recv,
    mean_send,
    mean_recv,
):
    me = lax.axis_index("member")
    shard = lax.axis_index("cell")
    rows, cells = prior_ref.shape
    ens = rows * groups
    width = cells // CHUNKS
    ncell = cells * shards
    peers = shards - 1
    low = 1 - (2 * me) // groups
    end = (me == 0) | (me == groups - 1)
    helper = (me == 1) | (me == groups - 2)
    outward = 1 - 2 * low
    furthest = me + low * (groups - 1 - 2 * me)
    steps = CHUNKS + LAG * (groups - 1)

    def span(c):
        return pl.ds(c * width if isinstance(c, int) else pl.multiple_of(c * width, width), width)

    def hop(way, origin, c, own=False):
        target = me + 1 if way == 0 else me - 1
        block = gath.at[origin, :, span(c)]
        return pltpu.make_async_remote_copy(
            src_ref=prior_ref.at[:, span(c)] if own else block,
            dst_ref=block,
            send_sem=send_sem.at[way, origin, c],
            recv_sem=recv_sem.at[origin, c],
            device_id={"member": target},
            device_id_type=MESH,
        )

    def left_out(c):
        return c % THIRD == 1

    def to_helper(i, g):
        source = samples_ref if i == 0 else noise_ref.at[0]
        return pltpu.make_async_remote_copy(
            src_ref=source.at[:, span(THIRD * g + 1)],
            dst_ref=guest_in.at[i, :, span(g)],
            send_sem=in_send.at[i, g],
            recv_sem=in_recv.at[i, g],
            device_id={"member": me - outward},
            device_id_type=MESH,
        )

    def part_to_end(way=1):
        return pltpu.make_async_remote_copy(
            src_ref=guest_part.at[0],
            dst_ref=guest_part.at[1],
            send_sem=guest_send.at[0],
            recv_sem=guest_recv.at[0],
            device_id={"member": me + way * outward},
            device_id_type=MESH,
        )

    def weights_to_helper():
        return pltpu.make_async_remote_copy(
            src_ref=guest_weights.at[0],
            dst_ref=guest_weights.at[1],
            send_sem=guest_send.at[1],
            recv_sem=guest_recv.at[1],
            device_id={"member": me - outward},
            device_id_type=MESH,
        )

    def mean_to_end(g, way=1):
        return pltpu.make_async_remote_copy(
            src_ref=guest_out.at[:, span(g)],
            dst_ref=guest_mean.at[:, span(g)],
            send_sem=mean_send.at[g],
            recv_sem=mean_recv.at[g],
            device_id={"member": me + way * outward},
            device_id_type=MESH,
        )

    def to_peer(k):
        return pltpu.make_async_remote_copy(
            src_ref=outbox,
            dst_ref=inbox.at[k],
            send_sem=red_send.at[k],
            recv_sem=red_recv.at[k],
            device_id={"cell": (shard + k + 1) % shards},
            device_id_type=MESH,
        )

    loads = [
        pltpu.make_async_copy(prior_ref, gath.at[me], local_sem.at[0]),
        pltpu.make_async_copy(samples_ref, samples_v, local_sem.at[1]),
        pltpu.make_async_copy(noise_ref, noise_v, local_sem.at[2]),
        pltpu.make_async_copy(cells_ref, cells_v, local_sem.at[3]),
        pltpu.make_async_copy(values_ref, values_v, local_sem.at[4]),
        pltpu.make_async_copy(mask_ref, mask_v, local_sem.at[5]),
    ]
    for load in loads:
        load.start()

    barrier = pltpu.get_barrier_semaphore()

    @pl.when(me > 0)
    def _():
        pl.semaphore_signal(barrier, inc=1, device_id={"member": me - 1}, device_id_type=MESH)

    @pl.when(me < groups - 1)
    def _():
        pl.semaphore_signal(barrier, inc=1, device_id={"member": me + 1}, device_id_type=MESH)

    for k in range(peers):
        pl.semaphore_signal(
            barrier, inc=1, device_id={"cell": (shard + k + 1) % shards}, device_id_type=MESH
        )
    inner = (me > 0) & (me < groups - 1)

    @pl.when(inner)
    def _():
        pl.semaphore_wait(barrier, peers + 2)

    @pl.when(jnp.logical_not(inner))
    def _():
        pl.semaphore_wait(barrier, peers + 1)

    def goes(way, c):
        if way == 0:
            return (me < groups - 2) | ((me < groups - 1) & jnp.logical_not(left_out(c)))
        return (me > 1) | ((me > 0) & jnp.logical_not(left_out(c)))

    def send_own(c):
        for way in range(2):

            @pl.when(goes(way, c))
            def _(way=way):
                hop(way, me, c, own=True).start()

    def begin(c, _):
        send_own(c)
        return 0

    lax.fori_loop(0, AHEAD, begin, 0)

    @pl.when(end)
    def _():
        def give(g, _):
            to_helper(0, g).start()
            to_helper(1, g).start()
            return 0

        lax.fori_loop(0, GUEST, give, 0)

    for load in loads[3:]:
        load.wait()

    blocks = cells // LANES
    count_obs = cells_ref.shape[1]
    piece = min(OBS_CHUNK, count_obs)
    eye = lax.broadcasted_iota(jnp.int32, (blocks, blocks), 0) == lax.broadcasted_iota(
        jnp.int32, (blocks, blocks), 1
    )
    field_v[...] = jnp.zeros_like(field_v)
    for survey in range(cells_ref.shape[0]):

        def gather_obs(o, total, survey=survey):
            at = pl.ds(pl.multiple_of(o * piece, piece), piece)
            where = cells_v[survey : survey + 1, at] - shard * cells
            values = values_v[survey : survey + 1, at]
            block_of = where // LANES
            lane_of = where - block_of * LANES
            first = (
                lax.broadcasted_iota(jnp.int32, (blocks, piece), 0) == block_of
            )
            second = lax.broadcasted_iota(jnp.int32, (LANES, piece), 0) == lane_of
            one = values.astype(jnp.bfloat16).astype(jnp.float32)
            two = (values - one).astype(jnp.bfloat16).astype(jnp.float32)
            three = values - one - two
            left = jnp.where(first, 1.0, 0.0).astype(jnp.bfloat16)
            right = jnp.concatenate(
                [
                    jnp.where(second, part, 0.0).astype(jnp.bfloat16)
                    for part in (jnp.ones_like(values), one, two, three)
                ],
                axis=0,
            )
            return total + lax.dot_general(left, right, NT, preferred_element_type=jnp.float32)

        total = lax.fori_loop(
            0, count_obs // piece, gather_obs, jnp.zeros((blocks, 4 * LANES), jnp.float32)
        )
        flags = mask_v[survey : survey + 1, :].astype(jnp.float32)
        column = jnp.sum(jnp.where(eye, flags, 0.0), axis=1, keepdims=True)
        field_v[0] += column * total[:, :LANES]
        field_v[1] += column * (
            total[:, LANES : 2 * LANES]
            + total[:, 2 * LANES : 3 * LANES]
            + total[:, 3 * LANES : 4 * LANES]
        )

    loads[1].wait()
    loads[2].wait()
    _, _, keep0, obs0, pull0, spread0 = constants(0)
    _, _, keep1, obs1, pull1, spread1 = constants(1)

    def advance(state, fresh, precision, target):
        return (keep0 - obs0 * precision) * state + obs0 * target + spread0 * fresh

    def prepare(h, _):
        at = pl.ds(pl.multiple_of(h * LANES, LANES), LANES)
        precision = field_v[0, pl.ds(h, 1), :]
        target = field_v[1, pl.ds(h, 1), :]
        state = samples_v[:, at]
        moved = advance(state, noise_v[0, :, at], precision, target)
        factor = keep1 - obs1 * precision
        base_v[:, at] = factor * moved + obs1 * target + spread1 * noise_v[1, :, at]
        scale_v[:, at] = jnp.broadcast_to(pull0 * factor, (rows, LANES))
        high, low = split(jnp.concatenate([state, moved], axis=0))
        split_sy[: 2 * rows, at] = high
        split_sy[2 * rows :, at] = low
        return 0

    def prepare_guest(c):
        g = c // THIRD
        to_helper(0, g).wait_recv()
        to_helper(1, g).wait_recv()

        def one(k, _):
            h = c * (width // LANES) + k
            at = pl.ds(pl.multiple_of(g * width + k * LANES, LANES), LANES)
            precision = field_v[0, pl.ds(h, 1), :]
            target = field_v[1, pl.ds(h, 1), :]
            state = guest_in[0, :, at]
            moved = advance(state, guest_in[1, :, at], precision, target)
            high, low = split(jnp.concatenate([state, moved], axis=0))
            guest_sy[: 2 * rows, at] = high
            guest_sy[2 * rows :, at] = low
            return 0

        lax.fori_loop(0, width // LANES, one, 0)

    loads[0].wait()
    acc[...] = jnp.zeros_like(acc)
    guest_acc[...] = jnp.zeros_like(guest_acc)

    four = 4 * rows

    def products(c, guest):
        at = span(c)
        high, low = split(gath[:, :, at].reshape(ens, width))
        split_p[:ens, at] = high
        split_p[ens:, at] = low
        right = jnp.concatenate([high, low], axis=0)
        first = [split_sy[:, at], guest_sy[:, span(c // THIRD)]] if guest else [split_sy[:, at]]
        left = jnp.concatenate(first + [right], axis=0)
        total = guest_acc if guest else acc
        total[...] += lax.dot_general(left, right, NT, preferred_element_type=jnp.float32)

    def fold(sy, gram):
        part = jnp.concatenate(
            [sy[: 2 * rows] + sy[2 * rows :], gram[:ens] + gram[ens:]], axis=0
        )
        part = part[:, :ens] + part[:, ens:]
        half = part.shape[0] // 2
        return jnp.concatenate([part[:half], part[half:]], axis=1)

    def relay(c, d):
        missing = left_out(c)

        @pl.when((me - d >= 0) & ((me < groups - 1) | jnp.logical_not(missing)))
        def _():
            hop(1, me - d, c).wait_recv()

            @pl.when(goes(0, c))
            def _():
                hop(0, me - d, c).start()

        @pl.when((me + d < groups) & ((me > 0) | jnp.logical_not(missing)))
        def _():
            hop(0, me + d, c).wait_recv()

            @pl.when(goes(1, c))
            def _():
                hop(1, me + d, c).start()

    def step(t, _):
        @pl.when(t + AHEAD < CHUNKS)
        def _():
            send_own(t + AHEAD)

        for d in range(1, groups):
            c = t - LAG * d

            @pl.when((c >= 0) & (c < CHUNKS))
            def _(c=c, d=d):
                relay(c, d)

        @pl.when(t < CHUNKS)
        def _():
            per = width // LANES
            lax.fori_loop(t * per, t * per + per, prepare, 0)

        c = t - LAG * furthest

        @pl.when((c >= 0) & (c < CHUNKS))
        def _():
            missing = left_out(c)

            @pl.when(missing & helper)
            def _():
                prepare_guest(c)
                products(c, True)

                @pl.when(c == THIRD * GUEST - 2)
                def _():
                    guest_part[0] = fold(guest_acc[four : 2 * four], guest_acc[2 * four :])
                    part_to_end().start()

            @pl.when(jnp.logical_not(missing & (end | helper)))
            def _():
                products(c, False)

        return 0

    lax.fori_loop(0, steps, step, 0)

    late = [THIRD * g + 1 for g in range(SERVED, GUEST)]

    @pl.when(me == 1)
    def _():
        for c in late:
            for origin in range(1, groups):
                hop(1, origin, c).start()

    @pl.when(me == groups - 2)
    def _():
        for c in late:
            for origin in range(groups - 1):
                hop(0, origin, c).start()

    @pl.when(helper)
    def _():
        acc[:four] += guest_acc[:four]
        acc[four:] += guest_acc[2 * four :]

    outbox[...] = fold(acc[:four], acc[four:])

    @pl.when(end)
    def _():
        part_to_end(-1).wait_recv()
        outbox[...] += guest_part[1]

    for k in range(peers):
        to_peer(k).start()
    part = outbox[...]
    for k in range(peers):
        to_peer(k).wait_recv()
        part = part + inbox[k]
    part = jnp.concatenate([part[:, :ens], part[:, ens:]], axis=0)
    cross0 = part[:rows]
    cross1 = part[rows : 2 * rows]
    gram = part[2 * rows :]
    diagonal = lax.broadcasted_iota(jnp.int32, (ens, ens), 0) == lax.broadcasted_iota(
        jnp.int32, (ens, ens), 1
    )
    prior_sq = jnp.sum(jnp.where(diagonal, gram, 0.0), axis=0, keepdims=True)

    def weigh(step, cross):
        time_now, alpha = constants(step)[:2]
        dist = alpha * alpha * prior_sq - 2.0 * alpha * cross
        return softmax_rows(-dist / (2.0 * time_now * math.sqrt(ncell)))

    weights0 = weigh(0, cross0)
    cross1 = cross1 + pull0 * jnp.dot(
        weights0, gram, precision=lax.Precision.HIGHEST, preferred_element_type=jnp.float32
    )
    weights1 = weigh(1, cross1)
    weights = jnp.concatenate([weights0, weights1], axis=0)

    @pl.when(end)
    def _():
        guest_weights[0] = jnp.concatenate([weights, weights], axis=1)
        weights_to_helper().start()

    def stack(high, low):
        both = jnp.concatenate([high, low], axis=0)
        return both if both.shape[1] == 2 * ens else jnp.concatenate([both, both], axis=1)

    def means(both, c):
        at = span(c)
        mean = jnp.dot(both, split_p[:, at], preferred_element_type=jnp.float32)
        mean = mean[: 2 * rows] + mean[2 * rows :]
        return scale_v[:, at] * mean[:rows] + pull1 * mean[rows:]

    @pl.when(helper)
    def _():
        weights_to_helper().wait_recv()
        guest_both = stack(*split(guest_weights[1]))

        def serve(g, _):
            guest_out[:, span(g)] = means(guest_both, THIRD * g + 1)
            mean_to_end(g).start()
            return 0

        lax.fori_loop(0, SERVED, serve, 0)

    both = stack(*split(weights))

    def store(c):
        return pltpu.make_async_copy(
            result_v.at[:, span(c)], out_ref.at[:, span(c)], out_sem.at[c]
        )

    def finish(c, _):
        at = span(c)

        @pl.when(jnp.logical_not(end & left_out(c)))
        def _():
            result_v[:, at] = base_v[:, at] + means(both, c)
            store(c).start()

        return 0

    lax.fori_loop(0, CHUNKS, finish, 0)

    def drain(c, _):
        for origin in range(groups):

            @pl.when((origin <= me) & goes(0, c))
            def _(origin=origin):
                hop(0, origin, c).wait_send()

            @pl.when((origin >= me) & goes(1, c))
            def _(origin=origin):
                hop(1, origin, c).wait_send()

        return 0

    lax.fori_loop(0, CHUNKS, drain, 0)
    for k in range(peers):
        to_peer(k).wait_send()

    @pl.when(end)
    def _():
        def taken(g, _):
            to_helper(0, g).wait_send()
            to_helper(1, g).wait_send()
            return 0

        lax.fori_loop(0, GUEST, taken, 0)
        weights_to_helper().wait_send()


    @pl.when(end)
    def _():
        def receive(g, _):
            c = THIRD * g + 1
            mean_to_end(g, -1).wait_recv()
            result_v[:, span(c)] = base_v[:, span(c)] + guest_mean[:, span(g)]
            store(c).start()
            return 0

        for c in late:

            @pl.when(me == 0)
            def _(c=c):
                for origin in range(1, groups):
                    hop(0, origin, c).wait_recv()

            @pl.when(me == groups - 1)
            def _(c=c):
                for origin in range(groups - 1):
                    hop(1, origin, c).wait_recv()

            high, low = split(gath[:, :, span(c)].reshape(ens, width))
            split_p[:ens, span(c)] = high
            split_p[ens:, span(c)] = low
            result_v[:, span(c)] = base_v[:, span(c)] + means(both, c)
            store(c).start()
        lax.fori_loop(0, SERVED, receive, 0)

    @pl.when(helper)
    def _():
        def sent(g, _):
            mean_to_end(g).wait_send()
            return 0

        lax.fori_loop(0, SERVED, sent, 0)
        part_to_end().wait_send()

    def written(c, _):
        store(c).wait()
        return 0

    lax.fori_loop(0, CHUNKS, written, 0)

    @pl.when(me == 1)
    def _():
        for c in late:
            for origin in range(1, groups):
                hop(1, origin, c).wait_send()

    @pl.when(me == groups - 2)
    def _():
        for c in late:
            for origin in range(groups - 1):
                hop(0, origin, c).wait_send()


def per_device(prior, samples, noise, obs_cells, obs_values, seismic_mask):
    rows, cells = prior.shape
    groups = lax.axis_size("member")
    shards = lax.axis_size("cell")
    ens = rows * groups
    peers = shards - 1
    half = (2 * rows + ens) // 2
    held = GUEST * (cells // CHUNKS)
    hbm = pl.BlockSpec(memory_space=pltpu.HBM)
    f32 = jnp.float32
    operands = [
        pltpu.with_memory_space_constraint(x, pltpu.HBM)
        for x in (prior, samples, noise, obs_cells, obs_values, seismic_mask)
    ]
    return pl.pallas_call(
        functools.partial(kernel, groups, shards),
        out_shape=jax.ShapeDtypeStruct((rows, cells), f32),
        in_specs=[hbm] * 6,
        out_specs=pl.BlockSpec(memory_space=pl.ANY),
        scratch_shapes=[
            pltpu.VMEM(obs_cells.shape, jnp.int32),
            pltpu.VMEM(obs_values.shape, f32),
            pltpu.VMEM(seismic_mask.shape, jnp.int32),
            pltpu.VMEM((groups, rows, cells), f32),
            pltpu.VMEM((rows, cells), f32),
            pltpu.VMEM((STEPS, rows, cells), f32),
            pltpu.VMEM((4 * rows, cells), jnp.bfloat16),
            pltpu.VMEM((2 * ens, cells), jnp.bfloat16),
            pltpu.VMEM((rows, cells), f32),
            pltpu.VMEM((rows, cells), f32),
            pltpu.VMEM((rows, cells), f32),
            pltpu.VMEM((2, cells // LANES, LANES), f32),
            pltpu.VMEM((4 * rows + 2 * ens, 2 * ens), f32),
            pltpu.VMEM((peers, half, 2 * ens), f32),
            pltpu.VMEM((half, 2 * ens), f32),
            pltpu.SemaphoreType.DMA((6,)),
            pltpu.SemaphoreType.DMA((CHUNKS,)),
            pltpu.SemaphoreType.DMA((2, groups, CHUNKS)),
            pltpu.SemaphoreType.DMA((groups, CHUNKS)),
            pltpu.SemaphoreType.DMA((peers,)),
            pltpu.SemaphoreType.DMA((peers,)),
            pltpu.VMEM((2, rows, held), f32),
            pltpu.VMEM((4 * rows, held), jnp.bfloat16),
            pltpu.VMEM((rows, held), f32),
            pltpu.VMEM((rows, held), f32),
            pltpu.VMEM((8 * rows + 2 * ens, 2 * ens), f32),
            pltpu.VMEM((2, half, 2 * ens), f32),
            pltpu.VMEM((2, 2 * rows, 2 * ens), f32),
            pltpu.SemaphoreType.DMA((2, GUEST)),
            pltpu.SemaphoreType.DMA((2, GUEST)),
            pltpu.SemaphoreType.DMA((2,)),
            pltpu.SemaphoreType.DMA((2,)),
            pltpu.SemaphoreType.DMA((GUEST,)),
            pltpu.SemaphoreType.DMA((GUEST,)),
        ],
        compiler_params=pltpu.CompilerParams(
            collective_id=0, has_side_effects=True, vmem_limit_bytes=48 * 1024 * 1024
        ),
    )(*operands)


def solution(mesh):
    in_specs = (
        P("member", "cell"),
        P("member", "cell"),
        P(None, "member", "cell"),
        P(None, "cell"),
        P(None, "cell"),
        P(None, "cell"),
    )
    out_specs = P("member", "cell")
    return jax.shard_map(
        per_device, mesh=mesh, in_specs=in_specs, out_specs=out_specs, check_vma=False
    )
```

```python
import functools
import math

import jax
import jax.numpy as jnp
from jax import lax
from jax.experimental import pallas as pl
from jax.experimental.pallas import tpu as pltpu
from jax.sharding import PartitionSpec as P

STEPS = 2
LANES = 128
CHUNKS = 16
THIRD = 3
GUEST = CHUNKS // THIRD
SERVED = GUEST - 2
LAG = 2
AHEAD = 14
OBS_CHUNK = 512
MESH = pl.DeviceIdType.MESH
NT = (((1,), (1,)), ((), ()))


def constants(step):
    time_now = 0.6 - 0.1 * step
    alpha = 1.0 - 0.95 * time_now
    drift = -0.95 / alpha
    diffusion = 1.0 - 2.0 * drift * time_now
    keep = 1.0 - 0.1 * drift - 0.1 * diffusion / time_now
    obs = 0.1 * diffusion * (1.0 - time_now)
    pull = 0.1 * diffusion * alpha / time_now
    spread = math.sqrt(0.1 * diffusion)
    return time_now, alpha, keep, obs, pull, spread


def split(x):
    high = x.astype(jnp.bfloat16)
    low = (x - high.astype(jnp.float32)).astype(jnp.bfloat16)
    return high, low


def softmax_rows(logits):
    top = jnp.max(logits, axis=1, keepdims=True)
    e = jnp.exp(logits - top)
    return e / jnp.sum(e, axis=1, keepdims=True)


def kernel(
    groups,
    shards,
    prior_ref,
    samples_ref,
    noise_ref,
    cells_ref,
    values_ref,
    mask_ref,
    out_ref,
    cells_v,
    values_v,
    mask_v,
    gath,
    samples_v,
    noise_v,
    split_sy,
    split_p,
    base_v,
    scale_v,
    result_v,
    field_v,
    acc,
    inbox,
    outbox,
    local_sem,
    out_sem,
    send_sem,
    recv_sem,
    red_send,
    red_recv,
    guest_in,
    guest_sy,
    guest_out,
    guest_mean,
    guest_acc,
    guest_part,
    guest_weights,
    in_send,
    in_recv,
    guest_send,
    guest_recv,
    mean_send,
    mean_recv,
):
    me = lax.axis_index("member")
    shard = lax.axis_index("cell")
    rows, cells = prior_ref.shape
    ens = rows * groups
    width = cells // CHUNKS
    ncell = cells * shards
    peers = shards - 1
    low = 1 - (2 * me) // groups
    end = (me == 0) | (me == groups - 1)
    helper = (me == 1) | (me == groups - 2)
    outward = 1 - 2 * low
    furthest = me + low * (groups - 1 - 2 * me)
    steps = CHUNKS + LAG * (groups - 1)

    def span(c):
        return pl.ds(c * width if isinstance(c, int) else pl.multiple_of(c * width, width), width)

    def hop(way, origin, c, own=False):
        target = me + 1 if way == 0 else me - 1
        block = gath.at[origin, :, span(c)]
        return pltpu.make_async_remote_copy(
            src_ref=prior_ref.at[:, span(c)] if own else block,
            dst_ref=block,
            send_sem=send_sem.at[way, origin, c],
            recv_sem=recv_sem.at[origin, c],
            device_id={"member": target},
            device_id_type=MESH,
        )

    def left_out(c):
        return c % THIRD == 1

    def to_helper(i, g):
        source = samples_ref if i == 0 else noise_ref.at[0]
        return pltpu.make_async_remote_copy(
            src_ref=source.at[:, span(THIRD * g + 1)],
            dst_ref=guest_in.at[i, :, span(g)],
            send_sem=in_send.at[i, g],
            recv_sem=in_recv.at[i, g],
            device_id={"member": me - outward},
            device_id_type=MESH,
        )

    def part_to_end(way=1):
        return pltpu.make_async_remote_copy(
            src_ref=guest_part.at[0],
            dst_ref=guest_part.at[1],
            send_sem=guest_send.at[0],
            recv_sem=guest_recv.at[0],
            device_id={"member": me + way * outward},
            device_id_type=MESH,
        )

    def weights_to_helper():
        return pltpu.make_async_remote_copy(
            src_ref=guest_weights.at[0],
            dst_ref=guest_weights.at[1],
            send_sem=guest_send.at[1],
            recv_sem=guest_recv.at[1],
            device_id={"member": me - outward},
            device_id_type=MESH,
        )

    def mean_to_end(g, way=1):
        return pltpu.make_async_remote_copy(
            src_ref=guest_out.at[:, span(g)],
            dst_ref=guest_mean.at[:, span(g)],
            send_sem=mean_send.at[g],
            recv_sem=mean_recv.at[g],
            device_id={"member": me + way * outward},
            device_id_type=MESH,
        )

    def to_peer(k):
        return pltpu.make_async_remote_copy(
            src_ref=outbox,
            dst_ref=inbox.at[k],
            send_sem=red_send.at[k],
            recv_sem=red_recv.at[k],
            device_id={"cell": (shard + k + 1) % shards},
            device_id_type=MESH,
        )

    loads = [
        pltpu.make_async_copy(prior_ref, gath.at[me], local_sem.at[0]),
        pltpu.make_async_copy(samples_ref, samples_v, local_sem.at[1]),
        pltpu.make_async_copy(noise_ref, noise_v, local_sem.at[2]),
        pltpu.make_async_copy(cells_ref, cells_v, local_sem.at[3]),
        pltpu.make_async_copy(values_ref, values_v, local_sem.at[4]),
        pltpu.make_async_copy(mask_ref, mask_v, local_sem.at[5]),
    ]
    for load in loads:
        load.start()

    barrier = pltpu.get_barrier_semaphore()

    @pl.when(me > 0)
    def _():
        pl.semaphore_signal(barrier, inc=1, device_id={"member": me - 1}, device_id_type=MESH)

    @pl.when(me < groups - 1)
    def _():
        pl.semaphore_signal(barrier, inc=1, device_id={"member": me + 1}, device_id_type=MESH)

    for k in range(peers):
        pl.semaphore_signal(
            barrier, inc=1, device_id={"cell": (shard + k + 1) % shards}, device_id_type=MESH
        )
    inner = (me > 0) & (me < groups - 1)

    @pl.when(inner)
    def _():
        pl.semaphore_wait(barrier, peers + 2)

    @pl.when(jnp.logical_not(inner))
    def _():
        pl.semaphore_wait(barrier, peers + 1)

    def goes(way, c):
        if way == 0:
            return (me < groups - 2) | ((me < groups - 1) & jnp.logical_not(left_out(c)))
        return (me > 1) | ((me > 0) & jnp.logical_not(left_out(c)))

    def send_own(c):
        for way in range(2):

            @pl.when(goes(way, c))
            def _(way=way):
                hop(way, me, c, own=True).start()

    def begin(c, _):
        send_own(c)
        return 0

    lax.fori_loop(0, AHEAD, begin, 0)

    @pl.when(end)
    def _():
        def give(g, _):
            to_helper(0, g).start()
            to_helper(1, g).start()
            return 0

        lax.fori_loop(0, GUEST, give, 0)

    for load in loads[3:]:
        load.wait()

    blocks = cells // LANES
    count_obs = cells_ref.shape[1]
    piece = min(OBS_CHUNK, count_obs)
    eye = lax.broadcasted_iota(jnp.int32, (blocks, blocks), 0) == lax.broadcasted_iota(
        jnp.int32, (blocks, blocks), 1
    )
    field_v[...] = jnp.zeros_like(field_v)
    for survey in range(cells_ref.shape[0]):

        def gather_obs(o, total, survey=survey):
            at = pl.ds(pl.multiple_of(o * piece, piece), piece)
            where = cells_v[survey : survey + 1, at] - shard * cells
            values = values_v[survey : survey + 1, at]
            block_of = where // LANES
            lane_of = where - block_of * LANES
            first = (
                lax.broadcasted_iota(jnp.int32, (blocks, piece), 0) == block_of
            )
            second = lax.broadcasted_iota(jnp.int32, (LANES, piece), 0) == lane_of
            one = values.astype(jnp.bfloat16).astype(jnp.float32)
            two = (values - one).astype(jnp.bfloat16).astype(jnp.float32)
            three = values - one - two
            left = jnp.where(first, 1.0, 0.0).astype(jnp.bfloat16)
            right = jnp.concatenate(
                [
                    jnp.where(second, part, 0.0).astype(jnp.bfloat16)
                    for part in (jnp.ones_like(values), one, two, three)
                ],
                axis=0,
            )
            return total + lax.dot_general(left, right, NT, preferred_element_type=jnp.float32)

        total = lax.fori_loop(
            0, count_obs // piece, gather_obs, jnp.zeros((blocks, 4 * LANES), jnp.float32)
        )
        flags = mask_v[survey : survey + 1, :].astype(jnp.float32)
        column = jnp.sum(jnp.where(eye, flags, 0.0), axis=1, keepdims=True)
        field_v[0] += column * total[:, :LANES]
        field_v[1] += column * (
            total[:, LANES : 2 * LANES]
            + total[:, 2 * LANES : 3 * LANES]
            + total[:, 3 * LANES : 4 * LANES]
        )

    loads[1].wait()
    loads[2].wait()
    _, _, keep0, obs0, pull0, spread0 = constants(0)
    _, _, keep1, obs1, pull1, spread1 = constants(1)

    def advance(state, fresh, precision, target):
        return (keep0 - obs0 * precision) * state + obs0 * target + spread0 * fresh

    def prepare(h, _):
        at = pl.ds(pl.multiple_of(h * LANES, LANES), LANES)
        precision = field_v[0, pl.ds(h, 1), :]
        target = field_v[1, pl.ds(h, 1), :]
        state = samples_v[:, at]
        moved = advance(state, noise_v[0, :, at], precision, target)
        factor = keep1 - obs1 * precision
        base_v[:, at] = factor * moved + obs1 * target + spread1 * noise_v[1, :, at]
        scale_v[:, at] = jnp.broadcast_to(pull0 * factor, (rows, LANES))
        high, low = split(jnp.concatenate([state, moved], axis=0))
        split_sy[: 2 * rows, at] = high
        split_sy[2 * rows :, at] = low
        return 0

    def prepare_guest(c):
        g = c // THIRD
        to_helper(0, g).wait_recv()
        to_helper(1, g).wait_recv()

        def one(k, _):
            h = c * (width // LANES) + k
            at = pl.ds(pl.multiple_of(g * width + k * LANES, LANES), LANES)
            precision = field_v[0, pl.ds(h, 1), :]
            target = field_v[1, pl.ds(h, 1), :]
            state = guest_in[0, :, at]
            moved = advance(state, guest_in[1, :, at], precision, target)
            high, low = split(jnp.concatenate([state, moved], axis=0))
            guest_sy[: 2 * rows, at] = high
            guest_sy[2 * rows :, at] = low
            return 0

        lax.fori_loop(0, width // LANES, one, 0)

    loads[0].wait()
    acc[...] = jnp.zeros_like(acc)
    guest_acc[...] = jnp.zeros_like(guest_acc)

    four = 4 * rows

    def products(c, guest):
        at = span(c)
        high, low = split(gath[:, :, at].reshape(ens, width))
        split_p[:ens, at] = high
        split_p[ens:, at] = low
        right = jnp.concatenate([high, low], axis=0)
        first = [split_sy[:, at], guest_sy[:, span(c // THIRD)]] if guest else [split_sy[:, at]]
        left = jnp.concatenate(first + [right], axis=0)
        total = guest_acc if guest else acc
        total[...] += lax.dot_general(left, right, NT, preferred_element_type=jnp.float32)

    def fold(sy, gram):
        part = jnp.concatenate(
            [sy[: 2 * rows] + sy[2 * rows :], gram[:ens] + gram[ens:]], axis=0
        )
        part = part[:, :ens] + part[:, ens:]
        half = part.shape[0] // 2
        return jnp.concatenate([part[:half], part[half:]], axis=1)

    def relay(c, d):
        missing = left_out(c)

        @pl.when((me - d >= 0) & ((me < groups - 1) | jnp.logical_not(missing)))
        def _():
            hop(1, me - d, c).wait_recv()

            @pl.when(goes(0, c))
            def _():
                hop(0, me - d, c).start()

        @pl.when((me + d < groups) & ((me > 0) | jnp.logical_not(missing)))
        def _():
            hop(0, me + d, c).wait_recv()

            @pl.when(goes(1, c))
            def _():
                hop(1, me + d, c).start()

    def step(t, _):
        @pl.when(t + AHEAD < CHUNKS)
        def _():
            send_own(t + AHEAD)

        for d in range(1, groups):
            c = t - LAG * d

            @pl.when((c >= 0) & (c < CHUNKS))
            def _(c=c, d=d):
                relay(c, d)

        @pl.when(t < CHUNKS)
        def _():
            per = width // LANES
            lax.fori_loop(t * per, t * per + per, prepare, 0)

        c = t - LAG * furthest

        @pl.when((c >= 0) & (c < CHUNKS))
        def _():
            missing = left_out(c)

            @pl.when(missing & helper)
            def _():
                prepare_guest(c)
                products(c, True)

                @pl.when(c == THIRD * GUEST - 2)
                def _():
                    guest_part[0] = fold(guest_acc[four : 2 * four], guest_acc[2 * four :])
                    part_to_end().start()

            @pl.when(jnp.logical_not(missing & (end | helper)))
            def _():
                products(c, False)

        return 0

    lax.fori_loop(0, steps, step, 0)

    late = [THIRD * g + 1 for g in range(SERVED, GUEST)]

    @pl.when(me == 1)
    def _():
        for c in late:
            for origin in range(1, groups):
                hop(1, origin, c).start()

    @pl.when(me == groups - 2)
    def _():
        for c in late:
            for origin in range(groups - 1):
                hop(0, origin, c).start()

    @pl.when(helper)
    def _():
        acc[:four] += guest_acc[:four]
        acc[four:] += guest_acc[2 * four :]

    outbox[...] = fold(acc[:four], acc[four:])

    @pl.when(end)
    def _():
        part_to_end(-1).wait_recv()
        outbox[...] += guest_part[1]

    for k in range(peers):
        to_peer(k).start()
    part = outbox[...]
    for k in range(peers):
        to_peer(k).wait_recv()
        part = part + inbox[k]
    part = jnp.concatenate([part[:, :ens], part[:, ens:]], axis=0)
    cross0 = part[:rows]
    cross1 = part[rows : 2 * rows]
    gram = part[2 * rows :]
    diagonal = lax.broadcasted_iota(jnp.int32, (ens, ens), 0) == lax.broadcasted_iota(
        jnp.int32, (ens, ens), 1
    )
    prior_sq = jnp.sum(jnp.where(diagonal, gram, 0.0), axis=0, keepdims=True)

    def weigh(step, cross):
        time_now, alpha = constants(step)[:2]
        dist = alpha * alpha * prior_sq - 2.0 * alpha * cross
        return softmax_rows(-dist / (2.0 * time_now * math.sqrt(ncell)))

    weights0 = weigh(0, cross0)
    cross1 = cross1 + pull0 * jnp.dot(
        weights0, gram, precision=lax.Precision.HIGHEST, preferred_element_type=jnp.float32
    )
    weights1 = weigh(1, cross1)
    weights = jnp.concatenate([weights0, weights1], axis=0)

    @pl.when(end)
    def _():
        guest_weights[0] = jnp.concatenate([weights, weights], axis=1)
        weights_to_helper().start()

    def stack(high, low):
        both = jnp.concatenate([high, low], axis=0)
        return both if both.shape[1] == 2 * ens else jnp.concatenate([both, both], axis=1)

    def means(both, c):
        at = span(c)
        mean = jnp.dot(both, split_p[:, at], preferred_element_type=jnp.float32)
        mean = mean[: 2 * rows] + mean[2 * rows :]
        return scale_v[:, at] * mean[:rows] + pull1 * mean[rows:]

    @pl.when(helper)
    def _():
        weights_to_helper().wait_recv()
        guest_both = stack(*split(guest_weights[1]))

        def serve(g, _):
            guest_out[:, span(g)] = means(guest_both, THIRD * g + 1)
            mean_to_end(g).start()
            return 0

        lax.fori_loop(0, SERVED, serve, 0)

    both = stack(*split(weights))

    def store(c):
        return pltpu.make_async_copy(
            result_v.at[:, span(c)], out_ref.at[:, span(c)], out_sem.at[c]
        )

    def finish(c, _):
        at = span(c)

        @pl.when(jnp.logical_not(end & left_out(c)))
        def _():
            result_v[:, at] = base_v[:, at] + means(both, c)
            store(c).start()

        return 0

    lax.fori_loop(0, CHUNKS, finish, 0)

    def drain(c, _):
        for origin in range(groups):

            @pl.when((origin <= me) & goes(0, c))
            def _(origin=origin):
                hop(0, origin, c).wait_send()

            @pl.when((origin >= me) & goes(1, c))
            def _(origin=origin):
                hop(1, origin, c).wait_send()

        return 0

    lax.fori_loop(0, CHUNKS, drain, 0)
    for k in range(peers):
        to_peer(k).wait_send()

    @pl.when(end)
    def _():
        def taken(g, _):
            to_helper(0, g).wait_send()
            to_helper(1, g).wait_send()
            return 0

        lax.fori_loop(0, GUEST, taken, 0)
        weights_to_helper().wait_send()


    @pl.when(end)
    def _():
        def receive(g, _):
            c = THIRD * g + 1
            mean_to_end(g, -1).wait_recv()
            result_v[:, span(c)] = base_v[:, span(c)] + guest_mean[:, span(g)]
            store(c).start()
            return 0

        for c in late:

            @pl.when(me == 0)
            def _(c=c):
                for origin in range(1, groups):
                    hop(0, origin, c).wait_recv()

            @pl.when(me == groups - 1)
            def _(c=c):
                for origin in range(groups - 1):
                    hop(1, origin, c).wait_recv()

            high, low = split(gath[:, :, span(c)].reshape(ens, width))
            split_p[:ens, span(c)] = high
            split_p[ens:, span(c)] = low
            result_v[:, span(c)] = base_v[:, span(c)] + means(both, c)
            store(c).start()
        lax.fori_loop(0, SERVED, receive, 0)

    @pl.when(helper)
    def _():
        def sent(g, _):
            mean_to_end(g).wait_send()
            return 0

        lax.fori_loop(0, SERVED, sent, 0)
        part_to_end().wait_send()

    def written(c, _):
        store(c).wait()
        return 0

    lax.fori_loop(0, CHUNKS, written, 0)

    @pl.when(me == 1)
    def _():
        for c in late:
            for origin in range(1, groups):
                hop(1, origin, c).wait_send()

    @pl.when(me == groups - 2)
    def _():
        for c in late:
            for origin in range(groups - 1):
                hop(0, origin, c).wait_send()


def per_device(prior, samples, noise, obs_cells, obs_values, seismic_mask):
    rows, cells = prior.shape
    groups = lax.axis_size("member")
    shards = lax.axis_size("cell")
    ens = rows * groups
    peers = shards - 1
    half = (2 * rows + ens) // 2
    held = GUEST * (cells // CHUNKS)
    hbm = pl.BlockSpec(memory_space=pltpu.HBM)
    f32 = jnp.float32
    operands = [
        pltpu.with_memory_space_constraint(x, pltpu.HBM)
        for x in (prior, samples, noise, obs_cells, obs_values, seismic_mask)
    ]
    return pl.pallas_call(
        functools.partial(kernel, groups, shards),
        out_shape=jax.ShapeDtypeStruct((rows, cells), f32),
        in_specs=[hbm] * 6,
        out_specs=pl.BlockSpec(memory_space=pl.ANY),
        scratch_shapes=[
            pltpu.VMEM(obs_cells.shape, jnp.int32),
            pltpu.VMEM(obs_values.shape, f32),
            pltpu.VMEM(seismic_mask.shape, jnp.int32),
            pltpu.VMEM((groups, rows, cells), f32),
            pltpu.VMEM((rows, cells), f32),
            pltpu.VMEM((STEPS, rows, cells), f32),
            pltpu.VMEM((4 * rows, cells), jnp.bfloat16),
            pltpu.VMEM((2 * ens, cells), jnp.bfloat16),
            pltpu.VMEM((rows, cells), f32),
            pltpu.VMEM((rows, cells), f32),
            pltpu.VMEM((rows, cells), f32),
            pltpu.VMEM((2, cells // LANES, LANES), f32),
            pltpu.VMEM((4 * rows + 2 * ens, 2 * ens), f32),
            pltpu.VMEM((peers, half, 2 * ens), f32),
            pltpu.VMEM((half, 2 * ens), f32),
            pltpu.SemaphoreType.DMA((6,)),
            pltpu.SemaphoreType.DMA((CHUNKS,)),
            pltpu.SemaphoreType.DMA((2, groups, CHUNKS)),
            pltpu.SemaphoreType.DMA((groups, CHUNKS)),
            pltpu.SemaphoreType.DMA((peers,)),
            pltpu.SemaphoreType.DMA((peers,)),
            pltpu.VMEM((2, rows, held), f32),
            pltpu.VMEM((4 * rows, held), jnp.bfloat16),
            pltpu.VMEM((rows, held), f32),
            pltpu.VMEM((rows, held), f32),
            pltpu.VMEM((8 * rows + 2 * ens, 2 * ens), f32),
            pltpu.VMEM((2, half, 2 * ens), f32),
            pltpu.VMEM((2, 2 * rows, 2 * ens), f32),
            pltpu.SemaphoreType.DMA((2, GUEST)),
            pltpu.SemaphoreType.DMA((2, GUEST)),
            pltpu.SemaphoreType.DMA((2,)),
            pltpu.SemaphoreType.DMA((2,)),
            pltpu.SemaphoreType.DMA((GUEST,)),
            pltpu.SemaphoreType.DMA((GUEST,)),
        ],
        compiler_params=pltpu.CompilerParams(
            collective_id=0, has_side_effects=True, vmem_limit_bytes=48 * 1024 * 1024
        ),
    )(*operands)


def solution(mesh):
    in_specs = (
        P("member", "cell"),
        P("member", "cell"),
        P(None, "member", "cell"),
        P(None, "cell"),
        P(None, "cell"),
        P(None, "cell"),
    )
    out_specs = P("member", "cell")
    return jax.shard_map(
        per_device, mesh=mesh, in_specs=in_specs, out_specs=out_specs, check_vma=False
    )
```
